256 devices in a mesh: rep: 4 (over y), shard: 64 (over x, z, core).
Axes of the slice: x: 4, y: 4, z: 8, core: 2. Of those that a mesh axis runs over, the one named last changes fastest.
Arguments:
- grad: bfloat16 [48, 1024, 1024], P(None, 'shard', 'rep'), may hold values from -2 to 2
- first_moment: float32 [48, 1024, 1024], P(None, 'shard', 'rep'), may hold values from -2 to 2
- second_moment: float32 [48, 1024, 1024], P(None, 'shard', 'rep'), may hold values from 0.0001 to 0.001
- stat_left: float32 [64, 1024, 1024], P('shard', 'rep'), may hold values from -1 to 3
- stat_right: float32 [64, 1024, 1024], P('shard', 'rep'), may hold values from -1 to 3
- root_left: bfloat16 [64, 1024, 1024], P('shard', 'rep'), may hold values from -1 to 3
- root_right: bfloat16 [64, 1024, 1024], P('shard', None, 'rep'), may hold values from -1 to 3
- owner_slot: int32 [48], replicated, may hold values from 0 to 63, as said below
Outputs:
- update: bfloat16 [48, 1024, 1024], P(None, 'shard', 'rep')
- new_first: float32 [48, 1024, 1024], P(None, 'shard', 'rep')
- new_second: float32 [48, 1024, 1024], P(None, 'shard', 'rep')
- new_left: float32 [64, 1024, 1024], P('shard', 'rep')
- new_right: float32 [64, 1024, 1024], P('shard', 'rep')
The draws below stay inside these ranges and needn't reach their ends.
Inputs may be any that keep to these rules, and one draw needn't show every extreme that they name: `owner_slot`: no two blocks share a value; each device along `shard` holds one slot, and the block whose value is o is owned by device o along `shard`. Owners without a block hold slots that no block names.
All inputs are finite; a program needn't handle non-finite values.
Results may differ from the reference program's by a relative error of at most 0.012.
Values may be sent and summed in bfloat16 or wider, within the bound.
A program may use at most 64 MiB of HBM per device.

```python
import math
import jax
import jax.numpy as jnp
from jax import lax

B = 1024
NBLK = 48
SLOTS = 64


def rough_blocks(key, scale):
    key_rows, key_cols, key_gauss = jax.random.split(key, 3)
    low = math.log(0.3)
    high = math.log(3.0)
    row_scale = jnp.exp(jax.random.uniform(key_rows, (NBLK, B, 1), jnp.float32, low, high))
    col_scale = jnp.exp(jax.random.uniform(key_cols, (NBLK, 1, B), jnp.float32, low, high))
    gauss = jnp.clip(jax.random.normal(key_gauss, (NBLK, B, B), jnp.float32), -6.0, 6.0)
    noise = gauss
    return scale * noise * row_scale * col_scale


def symmetric_slots(key, diag_low, diag_high):
    key_gauss = jax.random.fold_in(key, 0)
    key_diag = jax.random.fold_in(key, 2)
    gauss = jnp.clip(jax.random.normal(key_gauss, (SLOTS, B, B), jnp.float32), -6.0, 6.0)
    noise = gauss
    noise = 0.5 * (noise + jnp.swapaxes(noise, 1, 2)) * 1.4142135 * 0.6 * B ** (-0.5)
    diag = jnp.exp(jax.random.uniform(key_diag, (SLOTS, B), jnp.float32, math.log(diag_low), math.log(diag_high)))
    return noise + jnp.eye(B, dtype=jnp.float32)[None, :, :] * diag[:, :, None]


def draw_grad(key, part):
    key = jax.random.fold_in(key, 11)
    values = rough_blocks(key, 0.03)
    return values.astype(jnp.bfloat16)


def draw_first_moment(key, part):
    key = jax.random.fold_in(key, 13)
    values = rough_blocks(key, 0.03)
    return values.astype(jnp.float32)


def draw_stat_left(key, part):
    key = jax.random.fold_in(key, 21)
    values = symmetric_slots(key, 0.5, 2.0)
    return values.astype(jnp.float32)


def draw_stat_right(key, part):
    key = jax.random.fold_in(key, 23)
    values = symmetric_slots(key, 0.5, 2.0)
    return values.astype(jnp.float32)


def draw_root_left(key, part):
    key = jax.random.fold_in(key, 29)
    values = symmetric_slots(key, 0.5, 2.0)
    return values.astype(jnp.bfloat16)


def draw_root_right(key, part):
    key = jax.random.fold_in(key, 31)
    values = symmetric_slots(key, 0.5, 2.0)
    return values.astype(jnp.bfloat16)


def draw_owner_slot(key, part):
    key = jax.random.fold_in(key, 5)
    key_middle, key_order = jax.random.split(key, 2)
    middle = jax.random.permutation(key_middle, SLOTS - 2).astype(jnp.int32) + 1
    chosen = jnp.concatenate([jnp.array([0, SLOTS - 1], dtype=jnp.int32), middle[:NBLK - 2]])
    block_order = jax.random.permutation(key_order, NBLK).astype(jnp.int32)
    return jnp.zeros((NBLK,), jnp.int32).at[block_order].set(chosen)


def level_of(rng, shape, cuts, least, high):
    loudness, own = 1.0, jax.random.fold_in(rng, 6)
    for position, shards_of in cuts:
        steps = jnp.exp(jax.random.uniform(jax.random.fold_in(own, position), (shards_of,), jnp.float32, least / len(cuts), high / len(cuts)))
        loudness = loudness * jnp.repeat(steps, shape[position] // shards_of).reshape([-1 if axis == position else 1 for axis in range(len(shape))])
    return loudness


def setup_inputs(seed: int = 0) -> dict:
    streams_of = jax.random.split(jax.random.key(seed), 9)
    grad = draw_grad(jax.random.fold_in(streams_of[8], 71), 0)
    first_moment = draw_first_moment(jax.random.fold_in(streams_of[8], 71), 0)
    second_moment = jnp.clip(jnp.exp(math.log(0.001) - 2.3025852 * jax.random.uniform(streams_of[2], (NBLK, B, B), jnp.float32) ** level_of(streams_of[2], (NBLK, B, B), ((1, 64), (2, 4)), -0.2, 0.2)), 0.0001, 0.001)
    stat_left = draw_stat_left(jax.random.fold_in(streams_of[8], 71), 0)
    stat_right = draw_stat_right(jax.random.fold_in(streams_of[8], 71), 0)
    root_left = draw_root_left(jax.random.fold_in(streams_of[8], 71), 0)
    root_right = draw_root_right(jax.random.fold_in(streams_of[8], 71), 0)
    owner_slot = draw_owner_slot(jax.random.fold_in(streams_of[8], 71), 0)
    return {"grad": grad, "first_moment": first_moment, "second_moment": second_moment, "stat_left": stat_left, "stat_right": stat_right, "root_left": root_left, "root_right": root_right, "owner_slot": owner_slot}


beta_one = 0.9
beta_two = 0.95
adam_eps = 1e-08
norm_eps = 1e-06

def reference(grad, first_moment, second_moment, stat_left, stat_right, root_left, root_right, owner_slot):
    grad_wide = grad.astype(jnp.float32)
    new_first = beta_one * first_moment + (1.0 - beta_one) * grad_wide
    new_second = beta_two * second_moment + (1.0 - beta_two) * grad_wide * grad_wide
    adam = new_first / (jnp.sqrt(new_second) + adam_eps)
    adam_sq = lax.optimization_barrier(jnp.sum(adam * adam, axis=(1, 2)))

    def one_block(index):
        matrix = grad[index]
        slot = owner_slot[index]
        left_root = lax.dynamic_index_in_dim(root_left, slot, 0, keepdims=False)
        right_root = lax.dynamic_index_in_dim(root_right, slot, 0, keepdims=False)
        gram_left = jnp.dot(matrix, matrix.T, preferred_element_type=jnp.float32)
        gram_right = jnp.dot(matrix.T, matrix, preferred_element_type=jnp.float32)
        left_product = jnp.dot(left_root, matrix, preferred_element_type=jnp.float32)
        precond = jnp.dot(left_product, right_root.astype(jnp.float32), preferred_element_type=jnp.float32).astype(jnp.bfloat16)
        return (gram_left, gram_right, precond)
    gram_left, gram_right, precond = lax.map(one_block, jnp.arange(grad.shape[0], dtype=jnp.int32))
    new_left = stat_left.at[owner_slot].add(gram_left)
    new_right = stat_right.at[owner_slot].add(gram_right)
    precond_wide = precond.astype(jnp.float32)
    precond_sq = lax.optimization_barrier(jnp.sum(precond_wide * precond_wide, axis=(1, 2)))
    factor = jnp.sqrt(adam_sq) / (jnp.sqrt(precond_sq) + norm_eps)
    update = (-factor[:, None, None] * precond_wide).astype(jnp.bfloat16)
    return (update, new_first, new_second, new_left, new_right)
```

```python
import functools

import jax
import jax.numpy as jnp
from jax import lax
from jax.experimental import pallas as pl
from jax.experimental.pallas import tpu as pltpu
from jax.sharding import PartitionSpec as P

beta_one = 0.9
beta_two = 0.95
adam_eps = 1e-08
norm_eps = 1e-06

MESH = pl.DeviceIdType.MESH
f32 = jnp.float32
bf16 = jnp.bfloat16

NX, NZ, NC, NY = 4, 8, 2, 4
NS = NX * NZ * NC
GROUP = NZ * NC
X_ORDER = (0, 1, 3, 2)


def remote(src, dst, send_sem, recv_sem, device):
    return pltpu.make_async_remote_copy(
        src_ref=src,
        dst_ref=dst,
        send_sem=send_sem,
        recv_sem=recv_sem,
        device_id=device,
        device_id_type=MESH,
    )


def await_bytes(ref, sem):
    pltpu.make_async_copy(ref, ref, sem).wait()


def rows_of(index, count):
    return pl.ds(pl.multiple_of(index * count, count), count)


class ColumnGather:
    def __init__(self, buf, rows, sems, r, s):
        self.buf, self.rows = buf, rows
        self.own_send, self.own_recv, self.fwd_send, self.fwd_recv = sems
        self.r, self.s = r, s
        self.up = lax.rem(r + 1, NY)
        self.down = lax.rem(r + NY - 1, NY)
        self.opposite = lax.rem(r + 2, NY)

    def own(self, k, way):
        ref = self.buf.at[self.r, self.rows[k]]
        target = (self.up, self.down)[way]
        return remote(ref, ref, self.own_send.at[way, k], self.own_recv.at[way, k], (target, self.s))

    def arrived(self, k, way):
        ref = self.buf.at[(self.down, self.up)[way], self.rows[k]]
        await_bytes(ref, self.own_recv.at[way, k])

    def forward(self, k):
        way = k % 2
        ref = self.buf.at[(self.down, self.up)[way], self.rows[k]]
        target = (self.up, self.down)[way]
        return remote(ref, ref, self.fwd_send.at[k], self.fwd_recv.at[k], (target, self.s))

    def send(self, k):
        self.own(k, 0).start()
        self.own(k, 1).start()

    def pass_on(self, k):
        self.arrived(k, 0)
        self.arrived(k, 1)
        self.forward(k).start()

    def last(self, k):
        ref = self.buf.at[self.opposite, self.rows[k]]
        await_bytes(ref, self.fwd_recv.at[k])

    def drain(self):
        for k in range(4):
            self.own(k, 0).wait_send()
            self.own(k, 1).wait_send()
            self.forward(k).wait_send()


class SmallSum:
    def __init__(self, buf, send_sem, recv_sem, r, s):
        self.buf, self.send_sem, self.recv_sem = buf, send_sem, recv_sem
        x, z, c = lax.div(s, GROUP), lax.rem(lax.div(s, NC), NZ), lax.rem(s, NC)
        self.stages = {
            "core": (0, NC, c, lambda p: (r, s - c + p)),
            "z": (NC, NZ, z, lambda p: (r, (x * NZ + p) * NC + c)),
            "x": (NC + NZ, NX, x, lambda p: (r, p * GROUP + lax.rem(s, GROUP))),
            "y": (NC + NZ + NX, NY, r, lambda p: (p, s)),
        }

    def start(self, stage, tile):
        base, count, me, where = self.stages[stage]
        number = tuple(self.stages).index(stage)
        self.buf[base + me] = tile
        for step in range(1, count):
            p = lax.rem(me + step, count)
            ref = self.buf.at[base + me]
            remote(ref, ref, self.send_sem.at[number], self.recv_sem.at[number], where(p)).start()

    def finish(self, stage):
        base, count, me, where = self.stages[stage]
        number = tuple(self.stages).index(stage)
        others = self.buf.at[pl.ds(base, count - 1)]
        await_bytes(others, self.recv_sem.at[number])
        await_bytes(others, self.send_sem.at[number])
        total = self.buf[base]
        for p in range(1, count):
            total = total + self.buf[base + p]
        return total


SMALL = NC + NZ + NX + NY


def kernel(
    owner, inv, grad, m1, m2, stat_l, stat_r, root_l, root_r,
    update_out, first_out, second_out, left_out, right_out,
    gv, m1v, m2v, slv, srv, rlf, rrv, outb, gc, tv, pv, rc2, upv, acc, small_a, small_p,
    in_sem, out_sem, bulk_send, bulk_recv, back_send, back_recv,
    g_os, g_or, g_fs, g_fr, l_os, l_or, l_fs, l_fr,
    sa_send, sa_recv, sp_send, sp_recv,
):
    r = lax.axis_index("rep")
    s = lax.axis_index("shard")
    x = lax.div(s, GROUP)
    zc = lax.rem(s, GROUP)
    nblk = gv.shape[0]

    def load(i, src, dst):
        return pltpu.make_async_copy(src, dst, in_sem.at[i])

    loads = (
        load(0, grad, gv),
        load(1, root_l, rlf.at[r]),
        load(2, m1, m1v),
        load(3, m2, m2v),
        load(4, root_r, rrv),
        load(5, stat_l, slv),
        load(6, stat_r, srv),
    )
    for copy in loads:
        copy.start()

    barrier = pltpu.get_barrier_semaphore()

    def greet(i, carry):
        pl.semaphore_signal(
            barrier, inc=1, device_id=(r, lax.rem(s + i, NS)), device_id_type=MESH
        )
        return carry

    lax.fori_loop(1, NS, greet, 0)
    for step in range(1, NY):
        pl.semaphore_signal(
            barrier, inc=1, device_id=(lax.rem(r + step, NY), s), device_id_type=MESH
        )

    loads[0].wait()

    def pick(slot, carry):
        outb[slot] = gv[jnp.maximum(inv[slot], 0)]
        return carry

    lax.fori_loop(0, NS, pick, 0, unroll=4)
    loads[1].wait()
    pl.semaphore_wait(barrier, NS - 1 + NY - 1)

    mine = gc.at[r, rows_of(s, 16)]
    pltpu.make_async_copy(outb.at[s], mine, bulk_recv.at[x]).start()

    def send_rows(dx):
        plane = lax.rem(x + dx, NX)

        def body(i, carry):
            peer = plane * GROUP + lax.rem(zc + i, GROUP)
            remote(outb.at[peer], mine, bulk_send, bulk_recv.at[x], (r, peer)).start()
            return carry

        lax.fori_loop(1 if dx == 0 else 0, GROUP, body, 0)

    quarter = GROUP * 16
    grads = ColumnGather(
        gc,
        [rows_of(lax.rem(x + NX - dx, NX), quarter) for dx in X_ORDER],
        (g_os, g_or, g_fs, g_fr), r, s,
    )
    lefts = ColumnGather(rlf, [pl.ds(64 * k, 64) for k in range(4)], (l_os, l_or, l_fs, l_fr), r, s)

    send_rows(X_ORDER[0])
    for k in range(4):
        lefts.send(k)
    for dx in X_ORDER[1:]:
        send_rows(dx)

    loads[2].wait()
    loads[3].wait()

    def adam(b, carry):
        g = gv[b].astype(f32)
        first = beta_one * m1v[b] + (1.0 - beta_one) * g
        second = beta_two * m2v[b] + (1.0 - beta_two) * g * g
        m1v[b] = first
        m2v[b] = second
        step = first / (jnp.sqrt(second) + adam_eps)
        step = step * step
        step = step[:, :128] + step[:, 128:]
        acc[pl.ds(b, 1), :] = jnp.sum(step, axis=0, keepdims=True)
        return carry

    lax.fori_loop(0, nblk, adam, 0, unroll=2)
    store_first = pltpu.make_async_copy(m1v, first_out, out_sem.at[0])
    store_second = pltpu.make_async_copy(m2v, second_out, out_sem.at[1])
    store_first.start()
    store_second.start()
    sums = jnp.sum(acc[...], axis=1, keepdims=True)
    lane = lax.broadcasted_iota(jnp.int32, (nblk, 128), 1)
    row = lax.broadcasted_iota(jnp.int32, (nblk, 128), 0)
    vec = jnp.sum(jnp.where(lane == row, sums, 0.0), axis=0, keepdims=True)
    vec = jnp.broadcast_to(vec, (8, 128))
    adam_sum = SmallSum(small_a, sa_send, sa_recv, r, s)
    adam_sum.start("core", vec)

    def group_in(k):
        plane = lax.rem(x + NX - X_ORDER[k], NX)
        await_bytes(gc.at[r, rows_of(plane, quarter)], bulk_recv.at[plane])

    group_in(0)
    grads.send(0)
    adam_sum.start("z", adam_sum.finish("core"))
    lefts.pass_on(0)
    lefts.pass_on(1)
    group_in(1)
    grads.send(1)
    adam_sum.start("x", adam_sum.finish("z"))
    lefts.pass_on(2)
    group_in(2)
    grads.send(2)
    lefts.pass_on(3)
    group_in(3)
    grads.send(3)
    adam_sum.start("y", adam_sum.finish("x"))
    for k in range(4):
        grads.pass_on(k)
    adam_sq = adam_sum.finish("y")
    for k in range(4):
        lefts.last(k)
    for k in range(4):
        grads.last(k)

    loads[4].wait()

    def right_rows(m, carry):
        rows = rows_of(m, 256)
        total = jnp.zeros((256, 256), f32)
        for q in range(NY):
            total += jnp.dot(gc[q, rows, :], rrv[pl.ds(256 * q, 256), :], preferred_element_type=f32)
        tv[rows, :] = total.astype(bf16)
        return carry

    lax.fori_loop(0, 4, right_rows, 0)

    def left_rows(m, total):
        part = jnp.dot(rlf[m], tv[...], preferred_element_type=f32).astype(bf16)
        pv[rows_of(m, 256), :] = part
        wide = part.astype(f32)
        return total + jnp.sum(wide * wide, axis=0, keepdims=True)

    norm = lax.fori_loop(0, 4, left_rows, jnp.zeros((1, 256), f32))
    norm = jnp.sum(norm, axis=1, keepdims=True)
    block = inv[s]
    lanes = lax.broadcasted_iota(jnp.int32, (8, 128), 1)
    spot = jnp.where(lanes == block, jnp.broadcast_to(norm, (8, 128)), 0.0)
    norm_sum = SmallSum(small_p, sp_send, sp_recv, r, s)
    norm_sum.start("y", spot)

    pltpu.make_async_copy(pv.at[rows_of(s, 16)], rc2.at[s], back_recv).start()
    for dx in X_ORDER[::-1]:
        plane = lax.rem(x + dx, NX)

        def body(i, carry, plane=plane):
            peer = plane * GROUP + lax.rem(zc + i, GROUP)
            remote(pv.at[rows_of(peer, 16)], rc2.at[s], back_send, back_recv, (r, peer)).start()
            return carry

        lax.fori_loop(1 if dx == 0 else 0, GROUP, body, 0)

    has = (block >= 0).astype(f32)
    loads[5].wait()
    loads[6].wait()
    norm_sum.start("core", norm_sum.finish("y"))

    def gram_left(j, carry):
        cols = rows_of(j, 256)
        total = jnp.zeros((256, 256), f32)
        for q in range(NY):
            total += lax.dot_general(
                gc[q, rows_of(r, 256), :], gc[q, cols, :], (((1,), (1,)), ((), ())),
                preferred_element_type=f32,
            )
        slv[:, cols] = slv[:, cols] + has * total
        return carry

    lax.fori_loop(0, 4, gram_left, 0)
    store_left = pltpu.make_async_copy(slv, left_out, out_sem.at[2])
    store_left.start()
    norm_sum.start("z", norm_sum.finish("core"))

    def gram_right(q, carry):
        cols = rows_of(q, 256)
        total = lax.dot_general(
            gc[r], gc[q], (((0,), (0,)), ((), ())), preferred_element_type=f32
        )
        srv[:, cols] = srv[:, cols] + has * total
        return carry

    lax.fori_loop(0, 4, gram_right, 0)
    store_right = pltpu.make_async_copy(srv, right_out, out_sem.at[3])
    store_right.start()
    norm_sum.start("x", norm_sum.finish("z"))
    norm_sq = norm_sum.finish("x")

    factor = -(jnp.sqrt(adam_sq) / (jnp.sqrt(norm_sq) + norm_eps))
    await_bytes(rc2, back_recv)
    for b in range(nblk):
        scale = jnp.broadcast_to(factor[0:1, b : b + 1], (16, 256))
        upv[b] = (scale * rc2[owner[b]].astype(f32)).astype(bf16)
    store_update = pltpu.make_async_copy(upv, update_out, out_sem.at[4])
    store_update.start()

    grads.drain()
    lefts.drain()
    sent = gc.at[0, pl.ds(0, (NS - 1) * 16)]
    await_bytes(sent, bulk_send)
    await_bytes(sent, back_send)
    store_first.wait()
    store_second.wait()
    store_left.wait()
    store_right.wait()
    store_update.wait()


def per_device(
    grad, first_moment, second_moment, stat_left, stat_right, root_left, root_right, owner_slot
):
    slots = jnp.arange(NS, dtype=jnp.int32)
    numbers = jnp.arange(1, owner_slot.shape[0] + 1, dtype=jnp.int32)
    inverse = jnp.sum(
        jnp.where(owner_slot[None, :] == slots[:, None], numbers[None, :], 0), axis=1
    ) - 1
    nblk, rows, cols = grad.shape
    span, width = stat_left.shape[1:]
    any_spec = pl.BlockSpec(memory_space=pl.ANY)
    smem_spec = pl.BlockSpec(memory_space=pltpu.SMEM)
    dma = pltpu.SemaphoreType.DMA
    gather_sems = [dma((2, 4)), dma((2, 4)), dma((4,)), dma((4,))]
    update, first, second, left, right = pl.pallas_call(
        kernel,
        out_shape=(
            jax.ShapeDtypeStruct(grad.shape, bf16),
            jax.ShapeDtypeStruct(grad.shape, f32),
            jax.ShapeDtypeStruct(grad.shape, f32),
            jax.ShapeDtypeStruct((span, width), f32),
            jax.ShapeDtypeStruct((span, width), f32),
        ),
        in_specs=[smem_spec] * 2 + [any_spec] * 7,
        out_specs=[any_spec] * 5,
        scratch_shapes=[
            pltpu.VMEM((nblk, rows, cols), bf16),
            pltpu.VMEM((nblk, rows, cols), f32),
            pltpu.VMEM((nblk, rows, cols), f32),
            pltpu.VMEM((span, width), f32),
            pltpu.VMEM((span, width), f32),
            pltpu.VMEM((NY, span, width), bf16),
            pltpu.VMEM((width, cols), bf16),
            pltpu.VMEM((NS, rows, cols), bf16),
            pltpu.VMEM((NY, width, cols), bf16),
            pltpu.VMEM((width, cols), bf16),
            pltpu.VMEM((width, cols), bf16),
            pltpu.VMEM((NS, rows, cols), bf16),
            pltpu.VMEM((nblk, rows, cols), bf16),
            pltpu.VMEM((nblk, 128), f32),
            pltpu.VMEM((SMALL, 8, 128), f32),
            pltpu.VMEM((SMALL, 8, 128), f32),
            dma((7,)),
            dma((5,)),
            dma,
            dma((NX,)),
            dma,
            dma,
            *gather_sems,
            *gather_sems,
            dma((4,)),
            dma((4,)),
            dma((4,)),
            dma((4,)),
        ],
        compiler_params=pltpu.CompilerParams(
            collective_id=0, has_side_effects=True, vmem_limit_bytes=32 * 1024 * 1024
        ),
    )(
        owner_slot, inverse, grad, first_moment, second_moment, stat_left[0], stat_right[0],
        root_left[0], root_right[0],
    )
    return (update, first, second, left[None], right[None])


def solution(mesh):
    placed = (
        P(None, "shard", "rep"),
        P(None, "shard", "rep"),
        P(None, "shard", "rep"),
        P("shard", "rep", None),
        P("shard", "rep", None),
        P("shard", "rep", None),
        P("shard", None, "rep"),
        P(),
    )
    return jax.shard_map(
        per_device,
        mesh=mesh,
        in_specs=placed,
        out_specs=(
            P(None, "shard", "rep"),
            P(None, "shard", "rep"),
            P(None, "shard", "rep"),
            P("shard", "rep", None),
            P("shard", "rep", None),
        ),
        check_vma=False,
    )
```

```python
import functools

import jax
import jax.numpy as jnp
from jax import lax
from jax.experimental import pallas as pl
from jax.experimental.pallas import tpu as pltpu
from jax.sharding import PartitionSpec as P

beta_one = 0.9
beta_two = 0.95
adam_eps = 1e-08
norm_eps = 1e-06

MESH = pl.DeviceIdType.MESH
f32 = jnp.float32
bf16 = jnp.bfloat16

NX, NZ, NC, NY = 4, 8, 2, 4
NS = NX * NZ * NC
GROUP = NZ * NC
X_ORDER = (0, 1, 3, 2)
Z_ORDER = (1, 3, 2, 0)


def remote(src, dst, send_sem, recv_sem, device):
    return pltpu.make_async_remote_copy(
        src_ref=src,
        dst_ref=dst,
        send_sem=send_sem,
        recv_sem=recv_sem,
        device_id=device,
        device_id_type=MESH,
    )


def await_bytes(ref, sem):
    pltpu.make_async_copy(ref, ref, sem).wait()


def rows_of(index, count):
    return pl.ds(pl.multiple_of(index * count, count), count)


class ColumnGather:
    def __init__(self, buf, rows, sems, r, s):
        self.buf, self.rows = buf, rows
        self.own_send, self.own_recv, self.fwd_send, self.fwd_recv = sems
        self.r, self.s = r, s
        self.up = lax.rem(r + 1, NY)
        self.down = lax.rem(r + NY - 1, NY)
        self.opposite = lax.rem(r + 2, NY)

    def own(self, k, way):
        ref = self.buf.at[self.r, self.rows[k]]
        target = (self.up, self.down)[way]
        return remote(ref, ref, self.own_send.at[way, k], self.own_recv.at[way, k], (target, self.s))

    def arrived(self, k, way):
        ref = self.buf.at[(self.down, self.up)[way], self.rows[k]]
        await_bytes(ref, self.own_recv.at[way, k])

    def forward(self, k):
        way = k % 2
        ref = self.buf.at[(self.down, self.up)[way], self.rows[k]]
        target = (self.up, self.down)[way]
        return remote(ref, ref, self.fwd_send.at[k], self.fwd_recv.at[k], (target, self.s))

    def send(self, k):
        self.own(k, 0).start()
        self.own(k, 1).start()

    def pass_on(self, k):
        self.arrived(k, 0)
        self.arrived(k, 1)
        self.forward(k).start()

    def last(self, k):
        ref = self.buf.at[self.opposite, self.rows[k]]
        await_bytes(ref, self.fwd_recv.at[k])

    def drain(self):
        for k in range(4):
            self.own(k, 0).wait_send()
            self.own(k, 1).wait_send()
            self.forward(k).wait_send()


class SmallSum:
    def __init__(self, buf, send_sem, recv_sem, r, s):
        self.buf, self.send_sem, self.recv_sem = buf, send_sem, recv_sem
        x, z, c = lax.div(s, GROUP), lax.rem(lax.div(s, NC), NZ), lax.rem(s, NC)
        self.stages = {
            "core": (0, NC, c, lambda p: (r, s - c + p)),
            "z": (NC, NZ, z, lambda p: (r, (x * NZ + p) * NC + c)),
            "x": (NC + NZ, NX, x, lambda p: (r, p * GROUP + lax.rem(s, GROUP))),
            "y": (NC + NZ + NX, NY, r, lambda p: (p, s)),
        }

    def start(self, stage, tile):
        base, count, me, where = self.stages[stage]
        number = tuple(self.stages).index(stage)
        self.buf[base + me] = tile
        for step in range(1, count):
            p = lax.rem(me + step, count)
            ref = self.buf.at[base + me]
            remote(ref, ref, self.send_sem.at[number], self.recv_sem.at[number], where(p)).start()

    def finish(self, stage):
        base, count, me, where = self.stages[stage]
        number = tuple(self.stages).index(stage)
        others = self.buf.at[pl.ds(base, count - 1)]
        await_bytes(others, self.recv_sem.at[number])
        await_bytes(others, self.send_sem.at[number])
        total = self.buf[base]
        for p in range(1, count):
            total = total + self.buf[base + p]
        return total


SMALL = NC + NZ + NX + NY


def kernel(
    inv, grad, m1, m2, stat_l, stat_r, root_l, root_r,
    returned, factor_out, first_out, second_out, left_out, right_out,
    gv, m1v, m2v, slv, srv, rlf, rrv, outb, gc, tv, pv, acc, small_a, small_p, norms, facv,
    in_sem, out_sem, bulk_send, bulk_recv, back_send, back_recv,
    g_os, g_or, g_fs, g_fr, l_os, l_or, l_fs, l_fr,
    sa_send, sa_recv, sp_send, sp_recv, norm_send, norm_recv,
):
    r = lax.axis_index("rep")
    s = lax.axis_index("shard")
    x = lax.div(s, GROUP)
    zc = lax.rem(s, GROUP)
    nblk = gv.shape[0]

    def load(i, src, dst):
        return pltpu.make_async_copy(src, dst, in_sem.at[i])

    loads = (
        load(0, grad, gv),
        load(1, root_l, rlf.at[r]),
        load(2, m1, m1v),
        load(3, m2, m2v),
        load(4, root_r, rrv),
        load(5, stat_l, slv),
        load(6, stat_r, srv),
    )
    for copy in loads:
        copy.start()

    barrier = pltpu.get_barrier_semaphore()

    def greet(i, carry):
        pl.semaphore_signal(
            barrier, inc=1, device_id=(r, lax.rem(s + i, NS)), device_id_type=MESH
        )
        return carry

    lax.fori_loop(1, NS, greet, 0)
    for step in range(1, NY):
        pl.semaphore_signal(
            barrier, inc=1, device_id=(lax.rem(r + step, NY), s), device_id_type=MESH
        )

    loads[0].wait()

    def pick(slot, carry):
        outb[slot] = gv[jnp.maximum(inv[slot], 0)]
        return carry

    lax.fori_loop(0, NS, pick, 0, unroll=4)
    loads[1].wait()
    pl.semaphore_wait(barrier, NS - 1 + NY - 1)

    mine = gc.at[r, rows_of(s, 16)]
    pltpu.make_async_copy(outb.at[s], mine, bulk_recv.at[x]).start()

    def send_rows(dx):
        plane = lax.rem(x + dx, NX)

        def body(i, carry):
            peer = plane * GROUP + lax.rem(zc + i, GROUP)
            remote(outb.at[peer], mine, bulk_send, bulk_recv.at[x], (r, peer)).start()
            return carry

        lax.fori_loop(1 if dx == 0 else 0, GROUP, body, 0)

    quarter = GROUP * 16
    planes = [lax.rem(x + NX - dx, NX) for dx in X_ORDER]
    grads = ColumnGather(
        gc, [rows_of(plane, quarter) for plane in planes], (g_os, g_or, g_fs, g_fr), r, s
    )
    parts = [lax.rem(lax.div(zc, 4) + dz, 4) for dz in Z_ORDER]
    lefts = ColumnGather(rlf, [rows_of(part, 64) for part in parts], (l_os, l_or, l_fs, l_fr), r, s)

    send_rows(X_ORDER[0])
    lefts.send(0)
    lefts.send(1)
    for dx in X_ORDER[1:]:
        send_rows(dx)

    loads[2].wait()
    loads[3].wait()

    def adam(b, carry):
        g = gv[b].astype(f32)
        first = beta_one * m1v[b] + (1.0 - beta_one) * g
        second = beta_two * m2v[b] + (1.0 - beta_two) * g * g
        m1v[b] = first
        m2v[b] = second
        step = first / (jnp.sqrt(second) + adam_eps)
        step = step * step
        step = step[:, :128] + step[:, 128:]
        acc[pl.ds(b, 1), :] = jnp.sum(step, axis=0, keepdims=True)
        return carry

    lax.fori_loop(0, nblk, adam, 0, unroll=2)
    store_first = pltpu.make_async_copy(m1v, first_out, out_sem.at[0])
    store_second = pltpu.make_async_copy(m2v, second_out, out_sem.at[1])
    store_first.start()
    store_second.start()
    sums = jnp.sum(acc[...], axis=1, keepdims=True)
    lane = lax.broadcasted_iota(jnp.int32, (nblk, 128), 1)
    row = lax.broadcasted_iota(jnp.int32, (nblk, 128), 0)
    vec = jnp.sum(jnp.where(lane == row, sums, 0.0), axis=0, keepdims=True)
    vec = jnp.broadcast_to(vec, (8, 128))
    adam_sum = SmallSum(small_a, sa_send, sa_recv, r, s)
    adam_sum.start("core", vec)

    def group_in(k):
        await_bytes(gc.at[r, rows_of(planes[k], quarter)], bulk_recv.at[planes[k]])

    group_in(0)
    grads.send(0)
    lefts.pass_on(0)
    lefts.pass_on(1)
    adam_sum.start("z", adam_sum.finish("core"))
    group_in(1)
    grads.send(1)
    grads.pass_on(0)
    adam_sum.start("x", adam_sum.finish("z"))
    group_in(2)
    grads.send(2)
    grads.pass_on(1)
    group_in(3)
    grads.send(3)
    adam_sum.start("y", adam_sum.finish("x"))
    grads.pass_on(2)
    grads.pass_on(3)
    lefts.send(2)
    lefts.send(3)
    adam_sq = adam_sum.finish("y")

    loads[4].wait()

    def right_rows(k):
        rows = rows_of(planes[k], quarter)
        total = jnp.zeros((quarter, 256), f32)
        for q in range(NY):
            total += jnp.dot(gc[q, rows, :], rrv[pl.ds(256 * q, 256), :], preferred_element_type=f32)
        tv[rows, :] = total.astype(bf16)

    for k in range(NX):
        grads.last(k)
        right_rows(k)

    def precondition(j):
        rows = rows_of(parts[j], 64)
        part = rlf[:, rows, :].reshape(256, 1024)
        part = jnp.dot(part, tv[...], preferred_element_type=f32).astype(bf16)
        pv[:, rows, :] = part.reshape(NX, 64, 256)

        def body(i, carry):
            plane = lax.rem(x + lax.div(i, 4), NX)
            place = 4 * parts[j] + lax.rem(zc + i, 4)
            remote(
                pv.at[plane, rows_of(place, 16)], returned.at[s], back_send, back_recv,
                (r, plane * GROUP + place),
            ).start()
            return carry

        first = 0
        if Z_ORDER[j] == 0:
            pltpu.make_async_copy(pv.at[x, rows_of(zc, 16)], returned.at[s], back_recv).start()
            first = 1
        lax.fori_loop(first, 16, body, 0)
        wide = part.astype(f32)
        return jnp.sum(wide * wide, axis=0, keepdims=True)

    has = (inv[s] >= 0).astype(f32)

    def gram_left(j, carry):
        cols = rows_of(j, 256)
        total = jnp.zeros((256, 256), f32)
        for q in range(NY):
            total += lax.dot_general(
                gc[q, rows_of(r, 256), :], gc[q, cols, :], (((1,), (1,)), ((), ())),
                preferred_element_type=f32,
            )
        slv[:, cols] = slv[:, cols] + has * total
        return carry

    def gram_right(q, carry):
        cols = rows_of(q, 256)
        total = lax.dot_general(
            gc[r], gc[q], (((0,), (0,)), ((), ())), preferred_element_type=f32
        )
        srv[:, cols] = srv[:, cols] + has * total
        return carry

    lefts.last(0)
    norm = precondition(0)
    lefts.last(1)
    norm += precondition(1)
    loads[5].wait()
    lax.fori_loop(0, 4, gram_left, 0)
    store_left = pltpu.make_async_copy(slv, left_out, out_sem.at[2])
    store_left.start()
    lefts.pass_on(2)
    loads[6].wait()
    lax.fori_loop(0, 4, gram_right, 0)
    store_right = pltpu.make_async_copy(srv, right_out, out_sem.at[3])
    store_right.start()
    lefts.pass_on(3)
    lefts.last(2)
    norm += precondition(2)
    lefts.last(3)
    norm += precondition(3)

    norm = jnp.sum(norm, axis=1, keepdims=True)
    lanes = lax.broadcasted_iota(jnp.int32, (8, 128), 1)
    spot = jnp.where(lanes == inv[s], jnp.broadcast_to(norm, (8, 128)), 0.0)
    norm_sum = SmallSum(small_p, sp_send, sp_recv, r, s)
    norm_sum.start("y", spot)
    norms[s] = norm_sum.finish("y")[:1]

    def tell(i, carry):
        ref = norms.at[s]
        remote(ref, ref, norm_send, norm_recv, (r, lax.rem(s + i, NS))).start()
        return carry

    lax.fori_loop(1, NS, tell, 0)

    grads.drain()
    lefts.drain()
    sent = gc.at[0, pl.ds(0, (NS - 1) * 16)]
    await_bytes(sent, bulk_send)
    await_bytes(sent, back_send)
    store_first.wait()
    store_second.wait()
    store_left.wait()
    store_right.wait()
    others = norms.at[pl.ds(0, NS - 1)]
    await_bytes(others, norm_send)
    await_bytes(others, norm_recv)
    norm_sq = jnp.sum(norms[...], axis=0)
    facv[...] = -(jnp.sqrt(adam_sq) / (jnp.sqrt(norm_sq) + norm_eps))
    store_factor = pltpu.make_async_copy(facv, factor_out, out_sem.at[4])
    store_factor.start()
    await_bytes(returned, back_recv)
    store_factor.wait()


def finish(
    owner, returned, factor, first, second, left, right,
    update_out, first_out, second_out, left_out, right_out,
    rows, facv, upv, m1v, m2v, slv, srv, in_sem, out_sem,
):
    chain = (
        (first, m1v, first_out), (second, m2v, second_out), (left, slv, left_out), (right, srv, right_out)
    )
    takes = [
        pltpu.make_async_copy(src, via, in_sem.at[2 + i]) for i, (src, via, _) in enumerate(chain)
    ]
    gives = [
        pltpu.make_async_copy(via, dst, out_sem.at[1 + i]) for i, (_, via, dst) in enumerate(chain)
    ]
    take = pltpu.make_async_copy(returned, rows, in_sem.at[0])
    take_factor = pltpu.make_async_copy(factor, facv, in_sem.at[1])
    take.start()
    take_factor.start()
    for copy in takes:
        copy.start()
    take_factor.wait()
    take.wait()
    scales = facv[...]
    for b in range(upv.shape[0]):
        scale = jnp.broadcast_to(scales[0:1, b : b + 1], upv.shape[1:])
        upv[b] = (scale * rows[owner[b]].astype(f32)).astype(bf16)
    give = pltpu.make_async_copy(upv, update_out, out_sem.at[0])
    give.start()
    for came, goes in zip(takes, gives):
        came.wait()
        goes.start()
    for copy in gives:
        copy.wait()
    give.wait()


def per_device(
    grad, first_moment, second_moment, stat_left, stat_right, root_left, root_right, owner_slot
):
    slots = jnp.arange(NS, dtype=jnp.int32)
    numbers = jnp.arange(1, owner_slot.shape[0] + 1, dtype=jnp.int32)
    inverse = jnp.sum(
        jnp.where(owner_slot[None, :] == slots[:, None], numbers[None, :], 0), axis=1
    ) - 1
    nblk, rows, cols = grad.shape
    span, width = stat_left.shape[1:]
    any_spec = pl.BlockSpec(memory_space=pl.ANY)
    smem_spec = pl.BlockSpec(memory_space=pltpu.SMEM)
    dma = pltpu.SemaphoreType.DMA
    gather_sems = [dma((2, 4)), dma((2, 4)), dma((4,)), dma((4,))]
    moments = [jax.ShapeDtypeStruct(grad.shape, f32)] * 2
    stats = [jax.ShapeDtypeStruct((span, width), f32)] * 2
    grant = 60 * 1024 * 1024
    results = pl.pallas_call(
        kernel,
        out_shape=(
            jax.ShapeDtypeStruct((NS, rows, cols), bf16),
            jax.ShapeDtypeStruct((8, 128), f32),
            *moments,
            *stats,
        ),
        in_specs=[smem_spec] + [any_spec] * 7,
        out_specs=[any_spec] * 6,
        scratch_shapes=[
            pltpu.VMEM((nblk, rows, cols), bf16),
            pltpu.VMEM((nblk, rows, cols), f32),
            pltpu.VMEM((nblk, rows, cols), f32),
            pltpu.VMEM((span, width), f32),
            pltpu.VMEM((span, width), f32),
            pltpu.VMEM((NY, span, width), bf16),
            pltpu.VMEM((width, cols), bf16),
            pltpu.VMEM((NS, rows, cols), bf16),
            pltpu.VMEM((NY, width, cols), bf16),
            pltpu.VMEM((width, cols), bf16),
            pltpu.VMEM((NX, width // NX, cols), bf16),
            pltpu.VMEM((nblk, 128), f32),
            pltpu.VMEM((SMALL, 8, 128), f32),
            pltpu.VMEM((SMALL, 8, 128), f32),
            pltpu.VMEM((NS, 1, 128), f32),
            pltpu.VMEM((8, 128), f32),
            dma((7,)),
            dma((5,)),
            dma,
            dma((NX,)),
            dma,
            dma,
            *gather_sems,
            *gather_sems,
            dma((4,)),
            dma((4,)),
            dma((4,)),
            dma((4,)),
            dma,
            dma,
        ],
        compiler_params=pltpu.CompilerParams(
            collective_id=0, has_side_effects=True, vmem_limit_bytes=grant
        ),
    )(
        inverse, grad, first_moment, second_moment, stat_left[0], stat_right[0],
        root_left[0], root_right[0],
    )
    update, first, second, left, right = pl.pallas_call(
        finish,
        out_shape=(jax.ShapeDtypeStruct(grad.shape, bf16), *moments, *stats),
        in_specs=[smem_spec] + [any_spec] * 6,
        out_specs=[any_spec] * 5,
        scratch_shapes=[
            pltpu.VMEM((NS, rows, cols), bf16),
            pltpu.VMEM((8, 128), f32),
            pltpu.VMEM((nblk, rows, cols), bf16),
            pltpu.VMEM((nblk, rows, cols), f32),
            pltpu.VMEM((nblk, rows, cols), f32),
            pltpu.VMEM((span, width), f32),
            pltpu.VMEM((span, width), f32),
            dma((6,)),
            dma((5,)),
        ],
        compiler_params=pltpu.CompilerParams(vmem_limit_bytes=grant),
    )(owner_slot, *results)
    return (update, first, second, left[None], right[None])


def solution(mesh):
    placed = (
        P(None, "shard", "rep"),
        P(None, "shard", "rep"),
        P(None, "shard", "rep"),
        P("shard", "rep", None),
        P("shard", "rep", None),
        P("shard", "rep", None),
        P("shard", None, "rep"),
        P(),
    )
    return jax.shard_map(
        per_device,
        mesh=mesh,
        in_specs=placed,
        out_specs=(
            P(None, "shard", "rep"),
            P(None, "shard", "rep"),
            P(None, "shard", "rep"),
            P("shard", "rep", None),
            P("shard", "rep", None),
        ),
        check_vma=False,
    )
```

```python
import functools

import jax
import jax.numpy as jnp
from jax import lax
from jax.experimental import pallas as pl
from jax.experimental.pallas import tpu as pltpu
from jax.sharding import PartitionSpec as P

beta_one = 0.9
beta_two = 0.95
adam_eps = 1e-08
norm_eps = 1e-06

MESH = pl.DeviceIdType.MESH
f32 = jnp.float32
bf16 = jnp.bfloat16

NX, NZ, NC, NY = 4, 8, 2, 4
NS = NX * NZ * NC
GROUP = NZ * NC
Z_NEAR = (0, 1, 7, 2, 6, 3, 5, 4)
Z_FAR = (2, 1, 3, 0)
EARLY, FILL, LAG = 3, 2, 2


def remote(src, dst, send_sem, recv_sem, device):
    return pltpu.make_async_remote_copy(
        src_ref=src,
        dst_ref=dst,
        send_sem=send_sem,
        recv_sem=recv_sem,
        device_id=device,
        device_id_type=MESH,
    )


def await_bytes(ref, sem):
    pltpu.make_async_copy(ref, ref, sem).wait()


def rows_of(index, count):
    return pl.ds(pl.multiple_of(index * count, count), count)


class ColumnGather:
    def __init__(self, buf, rows, sems, r, s):
        self.buf, self.rows = buf, rows
        self.own_send, self.own_recv, self.fwd_send, self.fwd_recv = sems
        self.r, self.s = r, s
        self.up = lax.rem(r + 1, NY)
        self.down = lax.rem(r + NY - 1, NY)
        self.opposite = lax.rem(r + 2, NY)

    def chunk(self, q, k):
        return self.buf.at[q, :, self.rows[k]]

    def own(self, k, way):
        ref = self.chunk(self.r, k)
        target = (self.up, self.down)[way]
        return remote(ref, ref, self.own_send.at[way, k], self.own_recv.at[way, k], (target, self.s))

    def arrived(self, k, way):
        await_bytes(self.chunk((self.down, self.up)[way], k), self.own_recv.at[way, k])

    def forward(self, k):
        way = k % 2
        ref = self.chunk((self.down, self.up)[way], k)
        target = (self.up, self.down)[way]
        return remote(ref, ref, self.fwd_send.at[k], self.fwd_recv.at[k], (target, self.s))

    def send(self, k):
        self.own(k, 0).start()
        self.own(k, 1).start()

    def pass_on(self, k):
        self.arrived(k, k % 2)
        self.forward(k).start()

    def last(self, k):
        self.arrived(k, 1 - k % 2)
        await_bytes(self.chunk(self.opposite, k), self.fwd_recv.at[k])

    def drain(self):
        for k in range(len(self.rows)):
            self.own(k, 0).wait_send()
            self.own(k, 1).wait_send()
            self.forward(k).wait_send()


class SmallSum:
    def __init__(self, buf, send_sem, recv_sem, r, s):
        self.buf, self.send_sem, self.recv_sem = buf, send_sem, recv_sem
        x, z, c = lax.div(s, GROUP), lax.rem(lax.div(s, NC), NZ), lax.rem(s, NC)
        self.stages = {
            "core": (0, NC, c, lambda p: (r, s - c + p)),
            "z": (NC, NZ, z, lambda p: (r, (x * NZ + p) * NC + c)),
            "x": (NC + NZ, NX, x, lambda p: (r, p * GROUP + lax.rem(s, GROUP))),
            "y": (NC + NZ + NX, NY, r, lambda p: (p, s)),
        }

    def start(self, stage, tile):
        base, count, me, where = self.stages[stage]
        number = tuple(self.stages).index(stage)
        self.buf[base + me] = tile
        for step in range(1, count):
            p = lax.rem(me + step, count)
            ref = self.buf.at[base + me]
            remote(ref, ref, self.send_sem.at[number], self.recv_sem.at[number], where(p)).start()

    def finish(self, stage):
        base, count, me, where = self.stages[stage]
        number = tuple(self.stages).index(stage)
        others = self.buf.at[pl.ds(base, count - 1)]
        await_bytes(others, self.recv_sem.at[number])
        await_bytes(others, self.send_sem.at[number])
        total = self.buf[base]
        for p in range(1, count):
            total = total + self.buf[base + p]
        return total


SMALL = NC + NZ + NX + NY


def kernel(
    inv, grad, m1, m2, stat_l, stat_r, root_l, root_r,
    returned, factor_out, first_out, second_out, left_out, right_out,
    gv, m1v, m2v, slv, srv, rlv, rrv, outb, gc, tv, pv, ship, acc, small_a, small_p, norms, facv,
    in_sem, out_sem, bulk_send, bulk_recv, back_send, back_recv,
    g_os, g_or, g_fs, g_fr, l_send, l_recv, r_send, r_recv, ship_send, ship_recv,
    sa_send, sa_recv, sp_send, sp_recv, norm_send, norm_recv,
):
    r = lax.axis_index("rep")
    s = lax.axis_index("shard")
    x = lax.div(s, GROUP)
    zc = lax.rem(s, GROUP)
    z, c = lax.div(zc, NC), lax.rem(zc, NC)
    nblk = gv.shape[0]
    side = lax.rem(r, 2)
    left_mate = r + 1 - 2 * side
    right_mate = NY - 1 - r
    base = r - side

    def load(i, src, dst):
        return pltpu.make_async_copy(src, dst, in_sem.at[i])

    loads = (
        load(0, grad, gv),
        load(1, root_l, rlv.at[side]),
        load(2, root_r, rrv.at[0]),
        load(3, m1, m1v),
        load(4, m2, m2v),
        load(5, stat_l, slv),
        load(6, stat_r, srv),
    )
    for copy in loads:
        copy.start()

    barrier = pltpu.get_barrier_semaphore()

    def greet(i, carry):
        pl.semaphore_signal(
            barrier, inc=1, device_id=(r, lax.rem(s + i, NS)), device_id_type=MESH
        )
        return carry

    lax.fori_loop(1, NS, greet, 0)
    for step in range(1, NY):
        pl.semaphore_signal(
            barrier, inc=1, device_id=(lax.rem(r + step, NY), s), device_id_type=MESH
        )

    loads[0].wait()

    def pick(slot, carry):
        outb[slot] = gv[jnp.maximum(inv[slot], 0)]
        return carry

    lax.fori_loop(0, NS, pick, 0, unroll=4)
    loads[1].wait()
    loads[2].wait()
    pl.semaphore_wait(barrier, NS - 1 + NY - 1)

    mine = gc.at[r, x, rows_of(zc, 16)]
    pltpu.make_async_copy(outb.at[s], mine, bulk_recv.at[z]).start()

    def send_rows(dz):
        there = lax.rem(z + dz, NZ) * NC

        def body(i, carry):
            peer = lax.rem(x + lax.div(i, NC), NX) * GROUP + there + lax.rem(c + i, NC)
            remote(outb.at[peer], mine, bulk_send, bulk_recv.at[z], (r, peer)).start()
            return carry

        lax.fori_loop(1 if dz == 0 else 0, NX * NC, body, 0)

    quarters = [rows_of(lax.rem(lax.div(z, 2) + dq, 4), 64) for dq in Z_FAR]

    def left_root(j, i):
        ref = rlv.at[i, quarters[j]]
        return remote(ref, ref, l_send.at[j], l_recv.at[j], (left_mate, s))

    def right_root(j):
        rows = pl.ds(256 * j, 256)
        return remote(
            rrv.at[0, rows], rrv.at[1, rows], r_send.at[j], r_recv.at[j], (right_mate, s)
        )

    def swap_roots(j):
        left_root(j, side).start()
        right_root(j).start()

    near = [lax.rem(z + NZ - dz, NZ) for dz in Z_NEAR]
    grads = ColumnGather(gc, [rows_of(other, 32) for other in near], (g_os, g_or, g_fs, g_fr), r, s)

    for dz in Z_NEAR[:EARLY]:
        send_rows(dz)
    for j in range(FILL):
        swap_roots(j)
    for dz in Z_NEAR[EARLY:]:
        send_rows(dz)

    loads[3].wait()
    loads[4].wait()

    def adam(b, carry):
        g = gv[b].astype(f32)
        first = beta_one * m1v[b] + (1.0 - beta_one) * g
        second = beta_two * m2v[b] + (1.0 - beta_two) * g * g
        m1v[b] = first
        m2v[b] = second
        step = first / (jnp.sqrt(second) + adam_eps)
        step = step * step
        step = step[:, :128] + step[:, 128:]
        acc[pl.ds(b, 1), :] = jnp.sum(step, axis=0, keepdims=True)
        return carry

    lax.fori_loop(0, nblk, adam, 0, unroll=2)
    store_first = pltpu.make_async_copy(m1v, first_out, out_sem.at[0])
    store_second = pltpu.make_async_copy(m2v, second_out, out_sem.at[1])
    store_first.start()
    store_second.start()
    sums = jnp.sum(acc[...], axis=1, keepdims=True)
    lane = lax.broadcasted_iota(jnp.int32, (nblk, 128), 1)
    row = lax.broadcasted_iota(jnp.int32, (nblk, 128), 0)
    vec = jnp.sum(jnp.where(lane == row, sums, 0.0), axis=0, keepdims=True)
    vec = jnp.broadcast_to(vec, (8, 128))
    adam_sum = SmallSum(small_a, sa_send, sa_recv, r, s)
    adam_sum.start("core", vec)

    for k in range(NZ):
        await_bytes(grads.chunk(r, k), bulk_recv.at[near[k]])
        grads.send(k)
        if k >= LAG:
            grads.pass_on(k - LAG)
        if k == 1:
            adam_sum.start("z", adam_sum.finish("core"))
        if k == 4:
            adam_sum.start("x", adam_sum.finish("z"))
        if k == 6:
            adam_sum.start("y", adam_sum.finish("x"))
    for k in range(NZ - LAG, NZ):
        grads.pass_on(k)
    for j in range(FILL, 4):
        swap_roots(j)

    def right_rows(k):
        total = jnp.zeros((NX * 32, 256), f32)
        for q in range(NY):
            part = gc[q, :, grads.rows[k], :].reshape(NX * 32, 256)
            total += jnp.dot(part, rrv[0, pl.ds(256 * q, 256), :], preferred_element_type=f32)
        tv[:, grads.rows[k], :] = total.astype(bf16).reshape(NX, 32, 256)

    for k in range(NZ):
        grads.last(k)
        right_rows(k)

    def give_back(plane, j):
        def body(i, carry):
            place = 4 * lax.rem(lax.div(z, 2) + Z_FAR[j], 4) + lax.rem(zc + i, 4)
            peer = plane * GROUP + place
            src = pv.at[plane, rows_of(place, 16)]
            dst = returned.at[s]

            @pl.when(peer != s)
            def _():
                remote(src, dst, back_send, back_recv, (r, peer)).start()

            @pl.when(peer == s)
            def _():
                pltpu.make_async_copy(src, dst, back_recv).start()

            return carry

        lax.fori_loop(0, 4, body, 0)

    def squares(part):
        wide = part.astype(f32)
        return jnp.sum(wide * wide, axis=0, keepdims=True)

    part = jnp.dot(rlv[side], tv[...].reshape(1024, 256), preferred_element_type=f32).astype(bf16)
    pv[r] = part
    for j in range(4):
        give_back(r, j)
    norm = squares(part)

    has = (inv[s] >= 0).astype(f32)

    def gram_left(j, carry):
        cols = rows_of(j, 256)
        total = jnp.zeros((256, 256), f32)
        for q in range(NY):
            total += lax.dot_general(
                gc[q, r], gc[q, j], (((1,), (1,)), ((), ())), preferred_element_type=f32
            )
        slv[:, cols] = slv[:, cols] + has * total
        return carry

    def gram_right(q, carry):
        cols = rows_of(q, 256)
        total = lax.dot_general(
            gc[r].reshape(1024, 256), gc[q].reshape(1024, 256), (((0,), (0,)), ((), ())),
            preferred_element_type=f32,
        )
        srv[:, cols] = srv[:, cols] + has * total
        return carry

    def mate_rows(j, norm):
        left_root(j, 1 - side).wait_recv()
        part = jnp.dot(
            rlv[1 - side, quarters[j], :], tv[...].reshape(1024, 256), preferred_element_type=f32
        ).astype(bf16)
        pv[left_mate, quarters[j], :] = part
        give_back(left_mate, j)
        return norm + squares(part)

    norm = mate_rows(0, norm)
    loads[5].wait()
    lax.fori_loop(0, 4, gram_left, 0)
    store_left = pltpu.make_async_copy(slv, left_out, out_sem.at[2])
    store_left.start()
    norm = mate_rows(1, norm)
    loads[6].wait()
    lax.fori_loop(0, 4, gram_right, 0)
    store_right = pltpu.make_async_copy(srv, right_out, out_sem.at[3])
    store_right.start()
    norm = mate_rows(2, norm)
    norm = mate_rows(3, norm)

    for j in range(4):
        right_root(j).wait_recv()

    def right_mate_rows(m, carry):
        total = jnp.zeros((256, 256), f32)
        for q in range(NY):
            total += jnp.dot(gc[q, m], rrv[1, pl.ds(256 * q, 256), :], preferred_element_type=f32)
        tv[m] = total.astype(bf16)
        return carry

    lax.fori_loop(0, NX, right_mate_rows, 0)

    def shipment(j):
        return remote(
            ship.at[:, quarters[j]], pv.at[pl.ds(base, 2), quarters[j]],
            ship_send.at[j], ship_recv.at[j], (right_mate, s),
        )

    for i in range(2):
        part = jnp.dot(rlv[i], tv[...].reshape(1024, 256), preferred_element_type=f32).astype(bf16)
        ship[i] = part
        norm += squares(part)
    for j in range(4):
        shipment(j).start()

    norm = jnp.sum(norm, axis=1, keepdims=True)
    lanes = lax.broadcasted_iota(jnp.int32, (8, 128), 1)
    spot = jnp.where(lanes == inv[s], jnp.broadcast_to(norm, (8, 128)), 0.0)
    norm_sum = SmallSum(small_p, sp_send, sp_recv, r, s)
    norm_sum.start("y", spot)
    norms[s] = norm_sum.finish("y")[:1]

    def tell(i, carry):
        ref = norms.at[s]
        remote(ref, ref, norm_send, norm_recv, (r, lax.rem(s + i, NS))).start()
        return carry

    lax.fori_loop(1, NS, tell, 0)
    for j in range(4):
        arriving = pv.at[pl.ds(2 - base, 2), quarters[j]]
        await_bytes(arriving, ship_recv.at[j])
        give_back(2 - base, j)
        give_back(3 - base, j)

    grads.drain()
    for j in range(4):
        left_root(j, side).wait_send()
        right_root(j).wait_send()
        shipment(j).wait_send()
    sent = outb.at[pl.ds(0, NS - 1)]
    await_bytes(sent, bulk_send)
    await_bytes(sent, back_send)
    store_first.wait()
    store_second.wait()
    store_left.wait()
    store_right.wait()
    adam_sq = adam_sum.finish("y")
    others = norms.at[pl.ds(0, NS - 1)]
    await_bytes(others, norm_send)
    await_bytes(others, norm_recv)
    norm_sq = jnp.sum(norms[...], axis=0)
    facv[...] = -(jnp.sqrt(adam_sq) / (jnp.sqrt(norm_sq) + norm_eps))
    store_factor = pltpu.make_async_copy(facv, factor_out, out_sem.at[4])
    store_factor.start()
    await_bytes(returned, back_recv)
    store_factor.wait()


def finish(
    owner, returned, factor, first, second, left, right,
    update_out, first_out, second_out, left_out, right_out,
    rows, facv, upv, m1v, m2v, slv, srv, in_sem, out_sem,
):
    chain = (
        (first, m1v, first_out), (second, m2v, second_out), (left, slv, left_out), (right, srv, right_out)
    )
    takes = [
        pltpu.make_async_copy(src, via, in_sem.at[2 + i]) for i, (src, via, _) in enumerate(chain)
    ]
    gives = [
        pltpu.make_async_copy(via, dst, out_sem.at[1 + i]) for i, (_, via, dst) in enumerate(chain)
    ]
    take = pltpu.make_async_copy(returned, rows, in_sem.at[0])
    take_factor = pltpu.make_async_copy(factor, facv, in_sem.at[1])
    take.start()
    take_factor.start()
    for copy in takes:
        copy.start()
    take_factor.wait()
    take.wait()
    scales = facv[...]
    for b in range(upv.shape[0]):
        scale = jnp.broadcast_to(scales[0:1, b : b + 1], upv.shape[1:])
        upv[b] = (scale * rows[owner[b]].astype(f32)).astype(bf16)
    give = pltpu.make_async_copy(upv, update_out, out_sem.at[0])
    give.start()
    for came, goes in zip(takes, gives):
        came.wait()
        goes.start()
    for copy in gives:
        copy.wait()
    give.wait()


def per_device(
    grad, first_moment, second_moment, stat_left, stat_right, root_left, root_right, owner_slot
):
    slots = jnp.arange(NS, dtype=jnp.int32)
    numbers = jnp.arange(1, owner_slot.shape[0] + 1, dtype=jnp.int32)
    inverse = jnp.sum(
        jnp.where(owner_slot[None, :] == slots[:, None], numbers[None, :], 0), axis=1
    ) - 1
    nblk, rows, cols = grad.shape
    span, width = stat_left.shape[1:]
    any_spec = pl.BlockSpec(memory_space=pl.ANY)
    smem_spec = pl.BlockSpec(memory_space=pltpu.SMEM)
    dma = pltpu.SemaphoreType.DMA
    moments = [jax.ShapeDtypeStruct(grad.shape, f32)] * 2
    stats = [jax.ShapeDtypeStruct((span, width), f32)] * 2
    grant = 60 * 1024 * 1024
    results = pl.pallas_call(
        kernel,
        out_shape=(
            jax.ShapeDtypeStruct((NS, rows, cols), bf16),
            jax.ShapeDtypeStruct((8, 128), f32),
            *moments,
            *stats,
        ),
        in_specs=[smem_spec] + [any_spec] * 7,
        out_specs=[any_spec] * 6,
        scratch_shapes=[
            pltpu.VMEM((nblk, rows, cols), bf16),
            pltpu.VMEM((nblk, rows, cols), f32),
            pltpu.VMEM((nblk, rows, cols), f32),
            pltpu.VMEM((span, width), f32),
            pltpu.VMEM((span, width), f32),
            pltpu.VMEM((2, span, width), bf16),
            pltpu.VMEM((2, width, cols), bf16),
            pltpu.VMEM((NS, rows, cols), bf16),
            pltpu.VMEM((NY, NX, width // NX, cols), bf16),
            pltpu.VMEM((NX, width // NX, cols), bf16),
            pltpu.VMEM((NX, width // NX, cols), bf16),
            pltpu.VMEM((2, width // NX, cols), bf16),
            pltpu.VMEM((nblk, 128), f32),
            pltpu.VMEM((SMALL, 8, 128), f32),
            pltpu.VMEM((SMALL, 8, 128), f32),
            pltpu.VMEM((NS, 1, 128), f32),
            pltpu.VMEM((8, 128), f32),
            dma((7,)),
            dma((5,)),
            dma,
            dma((NZ,)),
            dma,
            dma,
            dma((2, NZ)),
            dma((2, NZ)),
            dma((NZ,)),
            dma((NZ,)),
            *[dma((4,))] * 6,
            dma((4,)),
            dma((4,)),
            dma((4,)),
            dma((4,)),
            dma,
            dma,
        ],
        compiler_params=pltpu.CompilerParams(
            collective_id=0, has_side_effects=True, vmem_limit_bytes=grant
        ),
    )(
        inverse, grad, first_moment, second_moment, stat_left[0], stat_right[0],
        root_left[0], root_right[0],
    )
    update, first, second, left, right = pl.pallas_call(
        finish,
        out_shape=(jax.ShapeDtypeStruct(grad.shape, bf16), *moments, *stats),
        in_specs=[smem_spec] + [any_spec] * 6,
        out_specs=[any_spec] * 5,
        scratch_shapes=[
            pltpu.VMEM((NS, rows, cols), bf16),
            pltpu.VMEM((8, 128), f32),
            pltpu.VMEM((nblk, rows, cols), bf16),
            pltpu.VMEM((nblk, rows, cols), f32),
            pltpu.VMEM((nblk, rows, cols), f32),
            pltpu.VMEM((span, width), f32),
            pltpu.VMEM((span, width), f32),
            dma((6,)),
            dma((5,)),
        ],
        compiler_params=pltpu.CompilerParams(vmem_limit_bytes=grant),
    )(owner_slot, *results)
    return (update, first, second, left[None], right[None])


def solution(mesh):
    placed = (
        P(None, "shard", "rep"),
        P(None, "shard", "rep"),
        P(None, "shard", "rep"),
        P("shard", "rep", None),
        P("shard", "rep", None),
        P("shard", "rep", None),
        P("shard", None, "rep"),
        P(),
    )
    return jax.shard_map(
        per_device,
        mesh=mesh,
        in_specs=placed,
        out_specs=(
            P(None, "shard", "rep"),
            P(None, "shard", "rep"),
            P(None, "shard", "rep"),
            P("shard", "rep", None),
            P("shard", "rep", None),
        ),
        check_vma=False,
    )
```

```python
import functools

import jax
import jax.numpy as jnp
from jax import lax
from jax.experimental import pallas as pl
from jax.experimental.pallas import tpu as pltpu
from jax.sharding import PartitionSpec as P

beta_one = 0.9
beta_two = 0.95
adam_eps = 1e-08
norm_eps = 1e-06

MESH = pl.DeviceIdType.MESH
f32 = jnp.float32
bf16 = jnp.bfloat16

NX, NZ, NC, NY = 4, 8, 2, 4
NS = NX * NZ * NC
GROUP = NZ * NC
Z_NEAR = (0, 1, 7, 2, 6, 3, 5, 4)
Z_FAR = (2, 1, 3, 0)
EARLY, FILL_LEFT, FILL_RIGHT, LAG = 3, 3, 4, 2


def remote(src, dst, send_sem, recv_sem, device):
    return pltpu.make_async_remote_copy(
        src_ref=src,
        dst_ref=dst,
        send_sem=send_sem,
        recv_sem=recv_sem,
        device_id=device,
        device_id_type=MESH,
    )


def await_bytes(ref, sem):
    pltpu.make_async_copy(ref, ref, sem).wait()


def rows_of(index, count):
    return pl.ds(pl.multiple_of(index * count, count), count)


class ColumnGather:
    def __init__(self, buf, rows, sems, r, s):
        self.buf, self.rows = buf, rows
        self.own_send, self.own_recv, self.fwd_send, self.fwd_recv = sems
        self.r, self.s = r, s
        self.up = lax.rem(r + 1, NY)
        self.down = lax.rem(r + NY - 1, NY)
        self.opposite = lax.rem(r + 2, NY)

    def chunk(self, q, k):
        return self.buf.at[q, :, self.rows[k]]

    def own(self, k, way):
        ref = self.chunk(self.r, k)
        target = (self.up, self.down)[way]
        return remote(ref, ref, self.own_send.at[way, k], self.own_recv.at[way, k], (target, self.s))

    def arrived(self, k, way):
        await_bytes(self.chunk((self.down, self.up)[way], k), self.own_recv.at[way, k])

    def forward(self, k):
        way = k % 2
        ref = self.chunk((self.down, self.up)[way], k)
        target = (self.up, self.down)[way]
        return remote(ref, ref, self.fwd_send.at[k], self.fwd_recv.at[k], (target, self.s))

    def send(self, k):
        self.own(k, 0).start()
        self.own(k, 1).start()

    def pass_on(self, k):
        self.arrived(k, k % 2)
        self.forward(k).start()

    def last(self, k):
        self.arrived(k, 1 - k % 2)
        await_bytes(self.chunk(self.opposite, k), self.fwd_recv.at[k])

    def drain(self):
        for k in range(len(self.rows)):
            self.own(k, 0).wait_send()
            self.own(k, 1).wait_send()
            self.forward(k).wait_send()


class SmallSum:
    def __init__(self, buf, send_sem, recv_sem, r, s):
        self.buf, self.send_sem, self.recv_sem = buf, send_sem, recv_sem
        x, z, c = lax.div(s, GROUP), lax.rem(lax.div(s, NC), NZ), lax.rem(s, NC)
        self.stages = {
            "core": (0, NC, c, lambda p: (r, s - c + p)),
            "z": (NC, NZ, z, lambda p: (r, (x * NZ + p) * NC + c)),
            "x": (NC + NZ, NX, x, lambda p: (r, p * GROUP + lax.rem(s, GROUP))),
            "y": (NC + NZ + NX, NY, r, lambda p: (p, s)),
        }

    def start(self, stage, tile):
        base, count, me, where = self.stages[stage]
        number = tuple(self.stages).index(stage)
        self.buf[base + me] = tile
        for step in range(1, count):
            p = lax.rem(me + step, count)
            ref = self.buf.at[base + me]
            remote(ref, ref, self.send_sem.at[number], self.recv_sem.at[number], where(p)).start()

    def finish(self, stage):
        base, count, me, where = self.stages[stage]
        number = tuple(self.stages).index(stage)
        others = self.buf.at[pl.ds(base, count - 1)]
        await_bytes(others, self.recv_sem.at[number])
        await_bytes(others, self.send_sem.at[number])
        total = self.buf[base]
        for p in range(1, count):
            total = total + self.buf[base + p]
        return total


SMALL = NC + NZ + NX + NY


def kernel(
    owner, grad, m1, m2, stat_l, stat_r, root_l, root_r,
    returned, factor_out, first_out, second_out, left_out, right_out,
    gv, m1v, m2v, slv, srv, rlv, rrv, outb, gc, tv, tv2, pv, ship, acc, small_a, small_p, norms, facv,
    invv, inv, inv_sem, word, in_sem, out_sem, bulk_send, bulk_recv, back_send, back_recv,
    g_os, g_or, g_fs, g_fr, l_send, l_recv, r_send, r_recv, ship_send, ship_recv,
    sa_send, sa_recv, sp_send, sp_recv, norm_send, norm_recv,
):
    r = lax.axis_index("rep")
    s = lax.axis_index("shard")
    x = lax.div(s, GROUP)
    zc = lax.rem(s, GROUP)
    z, c = lax.div(zc, NC), lax.rem(zc, NC)
    nblk = gv.shape[0]
    side = lax.rem(r, 2)
    left_mate = r + 1 - 2 * side
    right_mate = NY - 1 - r
    base = r - side

    def load(i, src, dst):
        return pltpu.make_async_copy(src, dst, in_sem.at[i])

    loads = (
        load(0, grad, gv),
        load(1, root_l, rlv.at[side]),
        load(2, root_r, rrv.at[0]),
        load(3, m1, m1v),
        load(4, m2, m2v),
        load(5, stat_l, slv),
        load(6, stat_r, srv),
    )
    for copy in loads:
        copy.start()

    barrier = pltpu.get_barrier_semaphore()

    def at(dx, dz, other=0):
        there = lax.rem(x + dx + NX, NX) * GROUP + lax.rem(z + dz + NZ, NZ) * NC
        return (r, there + lax.rem(c + other, NC))

    hellos = [(lax.rem(r + step, NY), s) for step in range(1, NY)]
    hellos += [at(0, 0, 1), at(1, 0), at(-1, 0), at(0, 1), at(0, -1)]
    for device in hellos:
        pl.semaphore_signal(barrier, inc=1, device_id=device, device_id_type=MESH)

    lanes = lax.broadcasted_iota(jnp.int32, (8, 128), 1)
    blocks = jnp.full((8, 128), -1, jnp.int32)
    for b in range(nblk):
        blocks = jnp.where(lanes == owner[b], b, blocks)
    invv[...] = blocks
    invert = pltpu.make_async_copy(invv, inv, inv_sem)
    invert.start()
    loads[0].wait()
    invert.wait()

    def pick(slot, carry):
        outb[slot] = gv[jnp.maximum(inv[0, slot], 0)]
        return carry

    lax.fori_loop(0, NS, pick, 0, unroll=4)
    loads[1].wait()
    loads[2].wait()
    pl.semaphore_wait(barrier, len(hellos))

    mine = gc.at[r, x, rows_of(zc, 16)]
    pltpu.make_async_copy(outb.at[s], mine, bulk_recv.at[z]).start()

    def send_rows(dz):
        there = lax.rem(z + dz, NZ) * NC

        def body(i, carry):
            peer = lax.rem(x + lax.div(i, NC), NX) * GROUP + there + lax.rem(c + i, NC)
            remote(outb.at[peer], mine, bulk_send, bulk_recv.at[z], (r, peer)).start()
            return carry

        lax.fori_loop(1 if dz == 0 else 0, NX * NC, body, 0)

    quarters = [rows_of(lax.rem(lax.div(z, 2) + dq, 4), 64) for dq in Z_FAR]

    def left_root(j, i):
        ref = rlv.at[i, quarters[j]]
        return remote(ref, ref, l_send.at[j], l_recv.at[j], (left_mate, s))

    def right_root(j):
        rows = pl.ds(256 * j, 256)
        return remote(
            rrv.at[0, rows], rrv.at[1, rows], r_send.at[j], r_recv.at[j], (right_mate, s)
        )

    near = [lax.rem(z + NZ - dz, NZ) for dz in Z_NEAR]
    grads = ColumnGather(gc, [rows_of(other, 32) for other in near], (g_os, g_or, g_fs, g_fr), r, s)

    for j in range(FILL_RIGHT):
        right_root(j).start()
        if j < FILL_LEFT:
            left_root(j, side).start()

    def say(i, device):
        pl.semaphore_signal(word.at[i], inc=1, device_id=device, device_id_type=MESH)

    def hear(i):
        pl.semaphore_wait(word.at[i], 1)

    say(0, at(1, 0))
    say(1, at(-1, 0))
    hear(0)
    hear(1)
    say(2, at(1, 0))
    hear(2)
    say(3, at(0, 1))
    say(4, at(0, -1))
    send_rows(0)
    for step in range(1, 4):
        hear(2 * step + 1)
        hear(2 * step + 2)
        say(2 * step + 3, at(0, 1))
        if step < 3:
            say(2 * step + 4, at(0, -1))
        send_rows(step)
        send_rows(NZ - step)
    hear(9)
    send_rows(4)

    loads[3].wait()
    loads[4].wait()

    def adam(b, carry):
        g = gv[b].astype(f32)
        first = beta_one * m1v[b] + (1.0 - beta_one) * g
        second = beta_two * m2v[b] + (1.0 - beta_two) * g * g
        m1v[b] = first
        m2v[b] = second
        step = first / (jnp.sqrt(second) + adam_eps)
        step = step * step
        step = step[:, :128] + step[:, 128:]
        acc[pl.ds(b, 1), :] = jnp.sum(step, axis=0, keepdims=True)
        return carry

    lax.fori_loop(0, nblk, adam, 0, unroll=2)
    store_first = pltpu.make_async_copy(m1v, first_out, out_sem.at[0])
    store_second = pltpu.make_async_copy(m2v, second_out, out_sem.at[1])
    store_first.start()
    store_second.start()
    sums = jnp.sum(acc[...], axis=1, keepdims=True)
    lane = lax.broadcasted_iota(jnp.int32, (nblk, 128), 1)
    row = lax.broadcasted_iota(jnp.int32, (nblk, 128), 0)
    vec = jnp.sum(jnp.where(lane == row, sums, 0.0), axis=0, keepdims=True)
    vec = jnp.broadcast_to(vec, (8, 128))
    adam_sum = SmallSum(small_a, sa_send, sa_recv, r, s)
    adam_sum.start("core", vec)

    for k in range(NZ):
        await_bytes(grads.chunk(r, k), bulk_recv.at[near[k]])
        grads.send(k)
        if k >= LAG:
            grads.pass_on(k - LAG)
        if k == 1:
            adam_sum.start("z", adam_sum.finish("core"))
        if k == 4:
            adam_sum.start("x", adam_sum.finish("z"))
        if k == 6:
            adam_sum.start("y", adam_sum.finish("x"))
    for k in range(NZ - LAG, NZ):
        grads.pass_on(k)
    for j in range(FILL_RIGHT, 4):
        right_root(j).start()
    for j in range(FILL_LEFT, 4):
        left_root(j, side).start()

    def right_rows(k):
        parts = [gc[q, :, grads.rows[k], :].reshape(NX * 32, 256) for q in range(NY)]
        for i, out in enumerate((tv, tv2)):
            total = jnp.zeros((NX * 32, 256), f32)
            for q in range(NY):
                total += jnp.dot(
                    parts[q], rrv[i, pl.ds(256 * q, 256), :], preferred_element_type=f32
                )
            out[:, grads.rows[k], :] = total.astype(bf16).reshape(NX, 32, 256)

    for j in range(4):
        right_root(j).wait_recv()
    for k in range(NZ):
        grads.last(k)
        right_rows(k)

    def give_back(plane, j):
        def body(i, carry):
            place = 4 * lax.rem(lax.div(z, 2) + Z_FAR[j], 4) + lax.rem(zc + i, 4)
            peer = plane * GROUP + place
            src = pv.at[plane, rows_of(place, 16)]
            dst = returned.at[s]

            @pl.when(peer != s)
            def _():
                remote(src, dst, back_send, back_recv, (r, peer)).start()

            @pl.when(peer == s)
            def _():
                pltpu.make_async_copy(src, dst, back_recv).start()

            return carry

        lax.fori_loop(0, 4, body, 0)

    def squares(part):
        wide = part.astype(f32)
        return jnp.sum(wide * wide, axis=0, keepdims=True)

    has = (inv[0, s] >= 0).astype(f32)

    def gram_left(j, carry):
        cols = rows_of(j, 256)
        total = jnp.zeros((256, 256), f32)
        for q in range(NY):
            total += lax.dot_general(
                gc[q, r], gc[q, j], (((1,), (1,)), ((), ())), preferred_element_type=f32
            )
        slv[:, cols] = slv[:, cols] + has * total
        return carry

    def gram_right(q, carry):
        cols = rows_of(q, 256)
        total = lax.dot_general(
            gc[r].reshape(1024, 256), gc[q].reshape(1024, 256), (((0,), (0,)), ((), ())),
            preferred_element_type=f32,
        )
        srv[:, cols] = srv[:, cols] + has * total
        return carry

    def product(left, right):
        return jnp.dot(
            left, right[...].reshape(1024, 256), preferred_element_type=f32
        ).astype(bf16)

    def shipment(i, j):
        plane = (r, left_mate)[i]
        return remote(
            ship.at[i, quarters[j]], pv.at[plane, quarters[j]], ship_send.at[i, j],
            ship_recv.at[i, j], (right_mate, s),
        )

    def shipped(i, j):
        plane = (right_mate, 3 - left_mate)[i]
        await_bytes(pv.at[plane, quarters[j]], ship_recv.at[i, j])
        give_back(plane, j)

    part = product(rlv[side], tv2)
    ship[0] = part
    for j in range(4):
        shipment(0, j).start()
    norm = squares(part)
    part = product(rlv[side], tv)
    pv[r] = part
    for j in range(4):
        give_back(r, j)
    norm += squares(part)

    def mate_rows(pair):
        for j in pair:
            left_root(j, 1 - side).wait_recv()
        left = jnp.concatenate([rlv[1 - side, quarters[j], :] for j in pair], axis=0)
        away = product(left, tv2)
        for n, j in enumerate(pair):
            ship[1, quarters[j], :] = away[64 * n : 64 * n + 64]
            shipment(1, j).start()
        here = product(left, tv)
        for n, j in enumerate(pair):
            pv[left_mate, quarters[j], :] = here[64 * n : 64 * n + 64]
            give_back(left_mate, j)
        return squares(away) + squares(here)

    norm += mate_rows((0, 1))
    norm += mate_rows((2, 3))

    norm = jnp.sum(norm, axis=1, keepdims=True)
    spot = jnp.where(lanes == inv[0, s], jnp.broadcast_to(norm, (8, 128)), 0.0)
    norm_sum = SmallSum(small_p, sp_send, sp_recv, r, s)
    norm_sum.start("y", spot)
    norms[s] = norm_sum.finish("y")[:1]

    def tell(i, carry):
        far = lax.rem(z + NZ // 2 + lax.div(i, NX * NC), NZ) * NC
        peer = lax.rem(x + 2 + lax.div(lax.rem(i, NX * NC), NC), NX) * GROUP + far + lax.rem(c + i, NC)
        ref = norms.at[s]

        @pl.when(peer != s)
        def _():
            remote(ref, ref, norm_send, norm_recv, (r, peer)).start()

        return carry

    lax.fori_loop(0, NS, tell, 0, unroll=4)
    for j in range(4):
        shipped(0, j)
    for j in range(4):
        shipped(1, j)

    loads[5].wait()
    lax.fori_loop(0, 4, gram_left, 0)
    store_left = pltpu.make_async_copy(slv, left_out, out_sem.at[2])
    store_left.start()
    loads[6].wait()
    lax.fori_loop(0, 4, gram_right, 0)
    store_right = pltpu.make_async_copy(srv, right_out, out_sem.at[3])
    store_right.start()

    grads.drain()
    for j in range(4):
        left_root(j, side).wait_send()
        right_root(j).wait_send()
        shipment(0, j).wait_send()
        shipment(1, j).wait_send()
    sent = outb.at[pl.ds(0, NS - 1)]
    await_bytes(sent, bulk_send)
    await_bytes(sent, back_send)
    store_first.wait()
    store_second.wait()
    store_left.wait()
    store_right.wait()
    adam_sq = adam_sum.finish("y")
    others = norms.at[pl.ds(0, NS - 1)]
    await_bytes(others, norm_send)
    await_bytes(others, norm_recv)
    norm_sq = jnp.sum(norms[...], axis=0)
    facv[...] = -(jnp.sqrt(adam_sq) / (jnp.sqrt(norm_sq) + norm_eps))
    store_factor = pltpu.make_async_copy(facv, factor_out, out_sem.at[4])
    store_factor.start()
    await_bytes(returned, back_recv)
    store_factor.wait()


def finish(
    owner, returned, factor, first, second, left, right,
    update_out, first_out, second_out, left_out, right_out,
    rows, facv, upv, m1v, m2v, slv, srv, in_sem, out_sem,
):
    chain = (
        (first, m1v, first_out), (second, m2v, second_out), (left, slv, left_out), (right, srv, right_out)
    )
    takes = [
        pltpu.make_async_copy(src, via, in_sem.at[2 + i]) for i, (src, via, _) in enumerate(chain)
    ]
    gives = [
        pltpu.make_async_copy(via, dst, out_sem.at[1 + i]) for i, (_, via, dst) in enumerate(chain)
    ]
    take = pltpu.make_async_copy(returned, rows, in_sem.at[0])
    take_factor = pltpu.make_async_copy(factor, facv, in_sem.at[1])
    take.start()
    take_factor.start()
    for copy in takes:
        copy.start()
    take_factor.wait()
    take.wait()
    scales = facv[...]
    for b in range(upv.shape[0]):
        scale = jnp.broadcast_to(scales[0:1, b : b + 1], upv.shape[1:])
        upv[b] = (scale * rows[owner[b]].astype(f32)).astype(bf16)
    give = pltpu.make_async_copy(upv, update_out, out_sem.at[0])
    give.start()
    for came, goes in zip(takes, gives):
        came.wait()
        goes.start()
    for copy in gives:
        copy.wait()
    give.wait()


def per_device(
    grad, first_moment, second_moment, stat_left, stat_right, root_left, root_right, owner_slot
):
    nblk, rows, cols = grad.shape
    span, width = stat_left.shape[1:]
    any_spec = pl.BlockSpec(memory_space=pl.ANY)
    smem_spec = pl.BlockSpec(memory_space=pltpu.SMEM)
    dma = pltpu.SemaphoreType.DMA
    moments = [jax.ShapeDtypeStruct(grad.shape, f32)] * 2
    stats = [jax.ShapeDtypeStruct((span, width), f32)] * 2
    grant = 60 * 1024 * 1024
    results = pl.pallas_call(
        kernel,
        out_shape=(
            jax.ShapeDtypeStruct((NS, rows, cols), bf16),
            jax.ShapeDtypeStruct((8, 128), f32),
            *moments,
            *stats,
        ),
        in_specs=[smem_spec] + [any_spec] * 7,
        out_specs=[any_spec] * 6,
        scratch_shapes=[
            pltpu.VMEM((nblk, rows, cols), bf16),
            pltpu.VMEM((nblk, rows, cols), f32),
            pltpu.VMEM((nblk, rows, cols), f32),
            pltpu.VMEM((span, width), f32),
            pltpu.VMEM((span, width), f32),
            pltpu.VMEM((2, span, width), bf16),
            pltpu.VMEM((2, width, cols), bf16),
            pltpu.VMEM((NS, rows, cols), bf16),
            pltpu.VMEM((NY, NX, width // NX, cols), bf16),
            pltpu.VMEM((NX, width // NX, cols), bf16),
            pltpu.VMEM((NX, width // NX, cols), bf16),
            pltpu.VMEM((NX, width // NX, cols), bf16),
            pltpu.VMEM((2, width // NX, cols), bf16),
            pltpu.VMEM((nblk, 128), f32),
            pltpu.VMEM((SMALL, 8, 128), f32),
            pltpu.VMEM((SMALL, 8, 128), f32),
            pltpu.VMEM((NS, 1, 128), f32),
            pltpu.VMEM((8, 128), f32),
            pltpu.VMEM((8, 128), jnp.int32),
            pltpu.SMEM((8, 128), jnp.int32),
            dma,
            pltpu.SemaphoreType.REGULAR((10,)),
            dma((7,)),
            dma((5,)),
            dma,
            dma((NZ,)),
            dma,
            dma,
            dma((2, NZ)),
            dma((2, NZ)),
            dma((NZ,)),
            dma((NZ,)),
            *[dma((4,))] * 4,
            *[dma((2, 4))] * 2,
            dma((4,)),
            dma((4,)),
            dma((4,)),
            dma((4,)),
            dma,
            dma,
        ],
        compiler_params=pltpu.CompilerParams(
            collective_id=0, has_side_effects=True, vmem_limit_bytes=grant
        ),
    )(
        owner_slot, grad, first_moment, second_moment, stat_left[0], stat_right[0],
        root_left[0], root_right[0],
    )
    update, first, second, left, right = pl.pallas_call(
        finish,
        out_shape=(jax.ShapeDtypeStruct(grad.shape, bf16), *moments, *stats),
        in_specs=[smem_spec] + [any_spec] * 6,
        out_specs=[any_spec] * 5,
        scratch_shapes=[
            pltpu.VMEM((NS, rows, cols), bf16),
            pltpu.VMEM((8, 128), f32),
            pltpu.VMEM((nblk, rows, cols), bf16),
            pltpu.VMEM((nblk, rows, cols), f32),
            pltpu.VMEM((nblk, rows, cols), f32),
            pltpu.VMEM((span, width), f32),
            pltpu.VMEM((span, width), f32),
            dma((6,)),
            dma((5,)),
        ],
        compiler_params=pltpu.CompilerParams(vmem_limit_bytes=grant),
    )(owner_slot, *results)
    return (update, first, second, left[None], right[None])


def solution(mesh):
    placed = (
        P(None, "shard", "rep"),
        P(None, "shard", "rep"),
        P(None, "shard", "rep"),
        P("shard", "rep", None),
        P("shard", "rep", None),
        P("shard", "rep", None),
        P("shard", None, "rep"),
        P(),
    )
    return jax.shard_map(
        per_device,
        mesh=mesh,
        in_specs=placed,
        out_specs=(
            P(None, "shard", "rep"),
            P(None, "shard", "rep"),
            P(None, "shard", "rep"),
            P("shard", "rep", None),
            P("shard", "rep", None),
        ),
        check_vma=False,
    )
```

```python
import functools

import jax
import jax.numpy as jnp
from jax import lax
from jax.experimental import pallas as pl
from jax.experimental.pallas import tpu as pltpu
from jax.sharding import PartitionSpec as P

beta_one = 0.9
beta_two = 0.95
adam_eps = 1e-08
norm_eps = 1e-06

MESH = pl.DeviceIdType.MESH
f32 = jnp.float32
bf16 = jnp.bfloat16

NX, NZ, NC, NY = 4, 8, 2, 4
NS = NX * NZ * NC
GROUP = NZ * NC
Z_NEAR = (0, 1, 7, 2, 6, 3, 5, 4)
Z_FAR = (2, 1, 3, 0)
LAG = 2


def remote(src, dst, send_sem, recv_sem, device):
    return pltpu.make_async_remote_copy(
        src_ref=src,
        dst_ref=dst,
        send_sem=send_sem,
        recv_sem=recv_sem,
        device_id=device,
        device_id_type=MESH,
    )


def await_bytes(ref, sem):
    pltpu.make_async_copy(ref, ref, sem).wait()


def rows_of(index, count):
    return pl.ds(pl.multiple_of(index * count, count), count)


class ColumnGather:
    def __init__(self, buf, rows, sems, r, s):
        self.buf, self.rows = buf, rows
        self.own_send, self.own_recv, self.fwd_send, self.fwd_recv = sems
        self.r, self.s = r, s
        self.up = lax.rem(r + 1, NY)
        self.down = lax.rem(r + NY - 1, NY)
        self.opposite = lax.rem(r + 2, NY)

    def chunk(self, q, k):
        return self.buf.at[q, :, self.rows[k]]

    def own(self, k, way):
        ref = self.chunk(self.r, k)
        target = (self.up, self.down)[way]
        return remote(ref, ref, self.own_send.at[way, k], self.own_recv.at[way, k], (target, self.s))

    def arrived(self, k, way):
        await_bytes(self.chunk((self.down, self.up)[way], k), self.own_recv.at[way, k])

    def forward(self, k):
        way = k % 2
        ref = self.chunk((self.down, self.up)[way], k)
        target = (self.up, self.down)[way]
        return remote(ref, ref, self.fwd_send.at[k], self.fwd_recv.at[k], (target, self.s))

    def send(self, k):
        self.own(k, 0).start()
        self.own(k, 1).start()

    def pass_on(self, k):
        self.arrived(k, k % 2)
        self.forward(k).start()

    def last(self, k):
        self.arrived(k, 1 - k % 2)
        await_bytes(self.chunk(self.opposite, k), self.fwd_recv.at[k])

    def drain(self):
        for k in range(len(self.rows)):
            self.own(k, 0).wait_send()
            self.own(k, 1).wait_send()
            self.forward(k).wait_send()


class SmallSum:
    def __init__(self, buf, send_sem, recv_sem, r, s):
        self.buf, self.send_sem, self.recv_sem = buf, send_sem, recv_sem
        x, z, c = lax.div(s, GROUP), lax.rem(lax.div(s, NC), NZ), lax.rem(s, NC)
        self.stages = {
            "core": (0, NC, c, lambda p: (r, s - c + p)),
            "z": (NC, NZ, z, lambda p: (r, (x * NZ + p) * NC + c)),
            "x": (NC + NZ, NX, x, lambda p: (r, p * GROUP + lax.rem(s, GROUP))),
            "y": (NC + NZ + NX, NY, r, lambda p: (p, s)),
        }

    def start(self, stage, tile):
        base, count, me, where = self.stages[stage]
        number = tuple(self.stages).index(stage)
        self.buf[base + me] = tile
        for step in range(1, count):
            p = lax.rem(me + step, count)
            ref = self.buf.at[base + me]
            remote(ref, ref, self.send_sem.at[number], self.recv_sem.at[number], where(p)).start()

    def finish(self, stage):
        base, count, me, where = self.stages[stage]
        number = tuple(self.stages).index(stage)
        others = self.buf.at[pl.ds(base, count - 1)]
        await_bytes(others, self.recv_sem.at[number])
        await_bytes(others, self.send_sem.at[number])
        total = self.buf[base]
        for p in range(1, count):
            total = total + self.buf[base + p]
        return total


SMALL = NC + NZ + NX + NY


def kernel(
    owner, grad, m1, m2, stat_l, stat_r, root_l, root_r,
    returned, factor_out, first_out, second_out, left_out, right_out,
    gv, m1v, m2v, slv, srv, rlv, rrv, outb, gc, tv, tv2, pv, ship, acc, small_a, small_p, norms, facv,
    invv, inv, inv_sem, word, in_sem, out_sem, bulk_send, bulk_recv, back_send, back_recv,
    g_os, g_or, g_fs, g_fr, l_send, l_recv, r_send, r_recv, ship_send, ship_recv,
    sa_send, sa_recv, sp_send, sp_recv, norm_send, norm_recv,
):
    r = lax.axis_index("rep")
    s = lax.axis_index("shard")
    x = lax.div(s, GROUP)
    zc = lax.rem(s, GROUP)
    z, c = lax.div(zc, NC), lax.rem(zc, NC)
    nblk = gv.shape[0]
    side = lax.rem(r, 2)
    left_mate = r + 1 - 2 * side
    right_mate = NY - 1 - r
    base = r - side

    def load(i, src, dst):
        return pltpu.make_async_copy(src, dst, in_sem.at[i])

    loads = (
        load(0, grad, gv),
        load(1, root_l, rlv.at[side]),
        load(2, root_r, rrv.at[0]),
        load(3, m1, m1v),
        load(4, m2, m2v),
        load(5, stat_l, slv),
        load(6, stat_r, srv),
    )
    for copy in loads:
        copy.start()

    barrier = pltpu.get_barrier_semaphore()

    def at(dx, dz, other=0):
        there = lax.rem(x + dx + NX, NX) * GROUP + lax.rem(z + dz + NZ, NZ) * NC
        return (r, there + lax.rem(c + other, NC))

    hellos = [(lax.rem(r + step, NY), s) for step in range(1, NY)]
    hellos += [at(dx, 0, other) for dx in range(NX) for other in range(NC) if dx or other]
    hellos += [at(0, 1), at(0, -1)]
    for device in hellos:
        pl.semaphore_signal(barrier, inc=1, device_id=device, device_id_type=MESH)

    lanes = lax.broadcasted_iota(jnp.int32, (8, 128), 1)
    blocks = jnp.full((8, 128), -1, jnp.int32)
    for b in range(nblk):
        blocks = jnp.where(lanes == owner[b], b, blocks)
    invv[...] = blocks
    invert = pltpu.make_async_copy(invv, inv, inv_sem)
    invert.start()
    loads[0].wait()
    invert.wait()

    def pick(slot, carry):
        outb[slot] = gv[jnp.maximum(inv[0, slot], 0)]
        return carry

    lax.fori_loop(0, NS, pick, 0, unroll=4)
    loads[1].wait()
    loads[2].wait()
    pl.semaphore_wait(barrier, len(hellos))

    mine = gc.at[r, x, rows_of(zc, 16)]
    pltpu.make_async_copy(outb.at[s], mine, bulk_recv.at[z]).start()

    def send_rows(dz):
        there = lax.rem(z + dz, NZ) * NC

        def body(i, carry):
            peer = lax.rem(x + lax.div(i, NC), NX) * GROUP + there + lax.rem(c + i, NC)
            remote(outb.at[peer], mine, bulk_send, bulk_recv.at[z], (r, peer)).start()
            return carry

        lax.fori_loop(1 if dz == 0 else 0, NX * NC, body, 0)

    quarters = [rows_of(lax.rem(lax.div(z, 2) + dq, 4), 64) for dq in Z_FAR]

    def left_root(j, i):
        ref = rlv.at[i, quarters[j]]
        return remote(ref, ref, l_send.at[j], l_recv.at[j], (left_mate, s))

    def right_root(j):
        rows = pl.ds(256 * j, 256)
        return remote(
            rrv.at[0, rows], rrv.at[1, rows], r_send.at[j], r_recv.at[j], (right_mate, s)
        )

    near = [lax.rem(z + NZ - dz, NZ) for dz in Z_NEAR]
    grads = ColumnGather(gc, [rows_of(other, 32) for other in near], (g_os, g_or, g_fs, g_fr), r, s)

    for j in range(4):
        right_root(j).start()
        left_root(j, side).start()

    loads[3].wait()
    loads[4].wait()

    def adam(b, carry):
        g = gv[b].astype(f32)
        first = beta_one * m1v[b] + (1.0 - beta_one) * g
        second = beta_two * m2v[b] + (1.0 - beta_two) * g * g
        m1v[b] = first
        m2v[b] = second
        step = first / (jnp.sqrt(second) + adam_eps)
        step = step * step
        step = step[:, :128] + step[:, 128:]
        acc[pl.ds(b, 1), :] = jnp.sum(step, axis=0, keepdims=True)
        return carry

    def say(i, device):
        pl.semaphore_signal(word.at[i], inc=1, device_id=device, device_id_type=MESH)

    def hear(i):
        pl.semaphore_wait(word.at[i], 1)

    say(0, at(0, 1))
    say(1, at(0, -1))
    send_rows(0)
    for step in range(1, 4):
        hear(2 * step - 2)
        hear(2 * step - 1)
        say(2 * step, at(0, 1))
        if step < 3:
            say(2 * step + 1, at(0, -1))
        send_rows(step)
        send_rows(NZ - step)
        lax.fori_loop((step - 1) * nblk // 3, step * nblk // 3, adam, 0, unroll=2)
    hear(6)
    send_rows(4)

    store_first = pltpu.make_async_copy(m1v, first_out, out_sem.at[0])
    store_second = pltpu.make_async_copy(m2v, second_out, out_sem.at[1])
    store_first.start()
    store_second.start()
    sums = jnp.sum(acc[...], axis=1, keepdims=True)
    lane = lax.broadcasted_iota(jnp.int32, (nblk, 128), 1)
    row = lax.broadcasted_iota(jnp.int32, (nblk, 128), 0)
    vec = jnp.sum(jnp.where(lane == row, sums, 0.0), axis=0, keepdims=True)
    vec = jnp.broadcast_to(vec, (8, 128))
    adam_sum = SmallSum(small_a, sa_send, sa_recv, r, s)
    adam_sum.start("core", vec)

    for k in range(NZ):
        await_bytes(grads.chunk(r, k), bulk_recv.at[near[k]])
        grads.send(k)
        if k >= LAG:
            grads.pass_on(k - LAG)
        if k == 1:
            adam_sum.start("z", adam_sum.finish("core"))
        if k == 4:
            adam_sum.start("x", adam_sum.finish("z"))
        if k == 6:
            adam_sum.start("y", adam_sum.finish("x"))
    for k in range(NZ - LAG, NZ):
        grads.pass_on(k)

    def right_rows(k):
        parts = [gc[q, :, grads.rows[k], :].reshape(NX * 32, 256) for q in range(NY)]
        for i, out in enumerate((tv, tv2)):
            total = jnp.zeros((NX * 32, 256), f32)
            for q in range(NY):
                total += jnp.dot(
                    parts[q], rrv[i, pl.ds(256 * q, 256), :], preferred_element_type=f32
                )
            out[:, grads.rows[k], :] = total.astype(bf16).reshape(NX, 32, 256)

    for j in range(4):
        right_root(j).wait_recv()
    for k in range(NZ):
        grads.last(k)
        right_rows(k)

    def give_back(plane, j):
        def body(i, carry):
            place = 4 * lax.rem(lax.div(z, 2) + Z_FAR[j], 4) + lax.rem(zc + i, 4)
            peer = plane * GROUP + place
            src = pv.at[plane, rows_of(place, 16)]
            dst = returned.at[s]

            @pl.when(peer != s)
            def _():
                remote(src, dst, back_send, back_recv, (r, peer)).start()

            @pl.when(peer == s)
            def _():
                pltpu.make_async_copy(src, dst, back_recv).start()

            return carry

        lax.fori_loop(0, 4, body, 0)

    def squares(part):
        wide = part.astype(f32)
        return jnp.sum(wide * wide, axis=0, keepdims=True)

    has = (inv[0, s] >= 0).astype(f32)

    def gram_left(j, carry):
        cols = rows_of(j, 256)
        total = jnp.zeros((256, 256), f32)
        for q in range(NY):
            total += lax.dot_general(
                gc[q, r], gc[q, j], (((1,), (1,)), ((), ())), preferred_element_type=f32
            )
        slv[:, cols] = slv[:, cols] + has * total
        return carry

    def gram_right(q, carry):
        cols = rows_of(q, 256)
        total = lax.dot_general(
            gc[r].reshape(1024, 256), gc[q].reshape(1024, 256), (((0,), (0,)), ((), ())),
            preferred_element_type=f32,
        )
        srv[:, cols] = srv[:, cols] + has * total
        return carry

    def product(left, right):
        return jnp.dot(
            left, right[...].reshape(1024, 256), preferred_element_type=f32
        ).astype(bf16)

    def shipment(i, j):
        plane = base + i
        return remote(
            ship.at[i, quarters[j]], pv.at[plane, quarters[j]], ship_send.at[i, j],
            ship_recv.at[i, j], (right_mate, s),
        )

    def shipped(i, j):
        plane = 2 - base + i
        await_bytes(pv.at[plane, quarters[j]], ship_recv.at[i, j])
        give_back(plane, j)

    for j in range(4):
        left_root(j, 1 - side).wait_recv()
    left = rlv[...].reshape(512, 1024)
    part = product(left, tv2)
    ship[0] = part[:256]
    ship[1] = part[256:]
    here = product(left, tv)
    pv[base] = here[:256]
    pv[base + 1] = here[256:]
    norm = squares(part) + squares(here)

    norm = jnp.sum(norm, axis=1, keepdims=True)
    spot = jnp.where(lanes == inv[0, s], jnp.broadcast_to(norm, (8, 128)), 0.0)
    norm_sum = SmallSum(small_p, sp_send, sp_recv, r, s)
    norm_sum.start("y", spot)
    for j in range(4):
        shipment(0, j).start()
        shipment(1, j).start()
    for j in range(2):
        give_back(base, j)
        give_back(base + 1, j)
    norms[s] = norm_sum.finish("y")[:1]

    def tell(i, carry):
        far = lax.rem(z + NZ // 2 + lax.div(i, NX * NC), NZ) * NC
        peer = lax.rem(x + 2 + lax.div(lax.rem(i, NX * NC), NC), NX) * GROUP + far + lax.rem(c + i, NC)
        ref = norms.at[s]

        @pl.when(peer != s)
        def _():
            remote(ref, ref, norm_send, norm_recv, (r, peer)).start()

        return carry

    lax.fori_loop(0, NS, tell, 0, unroll=4)
    for j in range(2, 4):
        give_back(base, j)
        give_back(base + 1, j)
    for j in range(4):
        shipped(0, j)
        shipped(1, j)

    loads[5].wait()
    lax.fori_loop(0, 4, gram_left, 0)
    store_left = pltpu.make_async_copy(slv, left_out, out_sem.at[2])
    store_left.start()
    loads[6].wait()
    lax.fori_loop(0, 4, gram_right, 0)
    store_right = pltpu.make_async_copy(srv, right_out, out_sem.at[3])
    store_right.start()

    grads.drain()
    for j in range(4):
        left_root(j, side).wait_send()
        right_root(j).wait_send()
        shipment(0, j).wait_send()
        shipment(1, j).wait_send()
    sent = outb.at[pl.ds(0, NS - 1)]
    await_bytes(sent, bulk_send)
    await_bytes(sent, back_send)
    store_first.wait()
    store_second.wait()
    store_left.wait()
    store_right.wait()
    adam_sq = adam_sum.finish("y")
    others = norms.at[pl.ds(0, NS - 1)]
    await_bytes(others, norm_send)
    await_bytes(others, norm_recv)
    norm_sq = jnp.sum(norms[...], axis=0)
    facv[...] = -(jnp.sqrt(adam_sq) / (jnp.sqrt(norm_sq) + norm_eps))
    store_factor = pltpu.make_async_copy(facv, factor_out, out_sem.at[4])
    store_factor.start()
    await_bytes(returned, back_recv)
    store_factor.wait()


def finish(
    owner, returned, factor, first, second, left, right,
    update_out, first_out, second_out, left_out, right_out,
    rows, facv, upv, m1v, m2v, slv, srv, in_sem, out_sem,
):
    chain = (
        (first, m1v, first_out), (second, m2v, second_out), (left, slv, left_out), (right, srv, right_out)
    )
    takes = [
        pltpu.make_async_copy(src, via, in_sem.at[2 + i]) for i, (src, via, _) in enumerate(chain)
    ]
    gives = [
        pltpu.make_async_copy(via, dst, out_sem.at[1 + i]) for i, (_, via, dst) in enumerate(chain)
    ]
    take = pltpu.make_async_copy(returned, rows, in_sem.at[0])
    take_factor = pltpu.make_async_copy(factor, facv, in_sem.at[1])
    take.start()
    take_factor.start()
    for copy in takes:
        copy.start()
    take_factor.wait()
    take.wait()
    scales = facv[...]
    for b in range(upv.shape[0]):
        scale = jnp.broadcast_to(scales[0:1, b : b + 1], upv.shape[1:])
        upv[b] = (scale * rows[owner[b]].astype(f32)).astype(bf16)
    give = pltpu.make_async_copy(upv, update_out, out_sem.at[0])
    give.start()
    for came, goes in zip(takes, gives):
        came.wait()
        goes.start()
    for copy in gives:
        copy.wait()
    give.wait()


def per_device(
    grad, first_moment, second_moment, stat_left, stat_right, root_left, root_right, owner_slot
):
    nblk, rows, cols = grad.shape
    span, width = stat_left.shape[1:]
    any_spec = pl.BlockSpec(memory_space=pl.ANY)
    smem_spec = pl.BlockSpec(memory_space=pltpu.SMEM)
    dma = pltpu.SemaphoreType.DMA
    moments = [jax.ShapeDtypeStruct(grad.shape, f32)] * 2
    stats = [jax.ShapeDtypeStruct((span, width), f32)] * 2
    grant = 60 * 1024 * 1024
    results = pl.pallas_call(
        kernel,
        out_shape=(
            jax.ShapeDtypeStruct((NS, rows, cols), bf16),
            jax.ShapeDtypeStruct((8, 128), f32),
            *moments,
            *stats,
        ),
        in_specs=[smem_spec] + [any_spec] * 7,
        out_specs=[any_spec] * 6,
        scratch_shapes=[
            pltpu.VMEM((nblk, rows, cols), bf16),
            pltpu.VMEM((nblk, rows, cols), f32),
            pltpu.VMEM((nblk, rows, cols), f32),
            pltpu.VMEM((span, width), f32),
            pltpu.VMEM((span, width), f32),
            pltpu.VMEM((2, span, width), bf16),
            pltpu.VMEM((2, width, cols), bf16),
            pltpu.VMEM((NS, rows, cols), bf16),
            pltpu.VMEM((NY, NX, width // NX, cols), bf16),
            pltpu.VMEM((NX, width // NX, cols), bf16),
            pltpu.VMEM((NX, width // NX, cols), bf16),
            pltpu.VMEM((NX, width // NX, cols), bf16),
            pltpu.VMEM((2, width // NX, cols), bf16),
            pltpu.VMEM((nblk, 128), f32),
            pltpu.VMEM((SMALL, 8, 128), f32),
            pltpu.VMEM((SMALL, 8, 128), f32),
            pltpu.VMEM((NS, 1, 128), f32),
            pltpu.VMEM((8, 128), f32),
            pltpu.VMEM((8, 128), jnp.int32),
            pltpu.SMEM((8, 128), jnp.int32),
            dma,
            pltpu.SemaphoreType.REGULAR((7,)),
            dma((7,)),
            dma((5,)),
            dma,
            dma((NZ,)),
            dma,
            dma,
            dma((2, NZ)),
            dma((2, NZ)),
            dma((NZ,)),
            dma((NZ,)),
            *[dma((4,))] * 4,
            *[dma((2, 4))] * 2,
            dma((4,)),
            dma((4,)),
            dma((4,)),
            dma((4,)),
            dma,
            dma,
        ],
        compiler_params=pltpu.CompilerParams(
            collective_id=0, has_side_effects=True, vmem_limit_bytes=grant
        ),
    )(
        owner_slot, grad, first_moment, second_moment, stat_left[0], stat_right[0],
        root_left[0], root_right[0],
    )
    update, first, second, left, right = pl.pallas_call(
        finish,
        out_shape=(jax.ShapeDtypeStruct(grad.shape, bf16), *moments, *stats),
        in_specs=[smem_spec] + [any_spec] * 6,
        out_specs=[any_spec] * 5,
        scratch_shapes=[
            pltpu.VMEM((NS, rows, cols), bf16),
            pltpu.VMEM((8, 128), f32),
            pltpu.VMEM((nblk, rows, cols), bf16),
            pltpu.VMEM((nblk, rows, cols), f32),
            pltpu.VMEM((nblk, rows, cols), f32),
            pltpu.VMEM((span, width), f32),
            pltpu.VMEM((span, width), f32),
            dma((6,)),
            dma((5,)),
        ],
        compiler_params=pltpu.CompilerParams(vmem_limit_bytes=grant),
    )(owner_slot, *results)
    return (update, first, second, left[None], right[None])


def solution(mesh):
    placed = (
        P(None, "shard", "rep"),
        P(None, "shard", "rep"),
        P(None, "shard", "rep"),
        P("shard", "rep", None),
        P("shard", "rep", None),
        P("shard", "rep", None),
        P("shard", None, "rep"),
        P(),
    )
    return jax.shard_map(
        per_device,
        mesh=mesh,
        in_specs=placed,
        out_specs=(
            P(None, "shard", "rep"),
            P(None, "shard", "rep"),
            P(None, "shard", "rep"),
            P("shard", "rep", None),
            P("shard", "rep", None),
        ),
        check_vma=False,
    )
```

```python
import functools

import jax
import jax.numpy as jnp
from jax import lax
from jax.experimental import pallas as pl
from jax.experimental.pallas import tpu as pltpu
from jax.sharding import PartitionSpec as P

beta_one = 0.9
beta_two = 0.95
adam_eps = 1e-08
norm_eps = 1e-06

MESH = pl.DeviceIdType.MESH
f32 = jnp.float32
bf16 = jnp.bfloat16

NX, NZ, NC, NY = 4, 8, 2, 4
NS = NX * NZ * NC
GROUP = NZ * NC
Z_NEAR = (0, 1, 7, 2, 6, 3, 5, 4)
Z_FAR = (2, 1, 3, 0)
LAG = 2


def remote(src, dst, send_sem, recv_sem, device):
    return pltpu.make_async_remote_copy(
        src_ref=src,
        dst_ref=dst,
        send_sem=send_sem,
        recv_sem=recv_sem,
        device_id=device,
        device_id_type=MESH,
    )


def await_bytes(ref, sem):
    pltpu.make_async_copy(ref, ref, sem).wait()


def rows_of(index, count):
    return pl.ds(pl.multiple_of(index * count, count), count)


class ColumnGather:
    def __init__(self, buf, rows, sems, r, s):
        self.buf, self.rows = buf, rows
        self.own_send, self.own_recv, self.fwd_send, self.fwd_recv = sems
        self.r, self.s = r, s
        self.up = lax.rem(r + 1, NY)
        self.down = lax.rem(r + NY - 1, NY)
        self.opposite = lax.rem(r + 2, NY)

    def chunk(self, q, k):
        return self.buf.at[q, :, self.rows[k]]

    def own(self, k, way):
        ref = self.chunk(self.r, k)
        target = (self.up, self.down)[way]
        return remote(ref, ref, self.own_send.at[way, k], self.own_recv.at[way, k], (target, self.s))

    def arrived(self, k, way):
        await_bytes(self.chunk((self.down, self.up)[way], k), self.own_recv.at[way, k])

    def forward(self, k):
        way = k % 2
        ref = self.chunk((self.down, self.up)[way], k)
        target = (self.up, self.down)[way]
        return remote(ref, ref, self.fwd_send.at[k], self.fwd_recv.at[k], (target, self.s))

    def send(self, k):
        self.own(k, 0).start()
        self.own(k, 1).start()

    def pass_on(self, k):
        self.arrived(k, k % 2)
        self.forward(k).start()

    def last(self, k):
        self.arrived(k, 1 - k % 2)
        await_bytes(self.chunk(self.opposite, k), self.fwd_recv.at[k])

    def drain(self):
        for k in range(len(self.rows)):
            self.own(k, 0).wait_send()
            self.own(k, 1).wait_send()
            self.forward(k).wait_send()


class SmallSum:
    def __init__(self, buf, send_sem, recv_sem, r, s):
        self.buf, self.send_sem, self.recv_sem = buf, send_sem, recv_sem
        x, z, c = lax.div(s, GROUP), lax.rem(lax.div(s, NC), NZ), lax.rem(s, NC)
        self.stages = {
            "core": (0, NC, c, lambda p: (r, s - c + p)),
            "z": (NC, NZ, z, lambda p: (r, (x * NZ + p) * NC + c)),
            "x": (NC + NZ, NX, x, lambda p: (r, p * GROUP + lax.rem(s, GROUP))),
            "y": (NC + NZ + NX, NY, r, lambda p: (p, s)),
        }

    def start(self, stage, tile):
        base, count, me, where = self.stages[stage]
        number = tuple(self.stages).index(stage)
        self.buf[base + me] = tile
        for step in range(1, count):
            p = lax.rem(me + step, count)
            ref = self.buf.at[base + me]
            remote(ref, ref, self.send_sem.at[number], self.recv_sem.at[number], where(p)).start()

    def finish(self, stage):
        base, count, me, where = self.stages[stage]
        number = tuple(self.stages).index(stage)
        others = self.buf.at[pl.ds(base, count - 1)]
        await_bytes(others, self.recv_sem.at[number])
        await_bytes(others, self.send_sem.at[number])
        total = self.buf[base]
        for p in range(1, count):
            total = total + self.buf[base + p]
        return total


SMALL = NC + NZ + NX + NY


def kernel(
    owner, grad, m1, m2, stat_l, stat_r, root_l, root_r,
    returned, factor_out, first_out, second_out, left_out, right_out,
    gv, m1v, m2v, slv, srv, rlv, rrv, outb, gc, tv, tv2, pv, ship, acc, small_a, small_p, norms, facv,
    invv, inv, inv_sem, word, in_sem, out_sem, bulk_send, bulk_recv, back_send, back_recv,
    g_os, g_or, g_fs, g_fr, l_send, l_recv, r_send, r_recv, ship_send, ship_recv,
    sa_send, sa_recv, sp_send, sp_recv, norm_send, norm_recv,
):
    r = lax.axis_index("rep")
    s = lax.axis_index("shard")
    x = lax.div(s, GROUP)
    zc = lax.rem(s, GROUP)
    z, c = lax.div(zc, NC), lax.rem(zc, NC)
    nblk = gv.shape[0]
    side = lax.rem(r, 2)
    left_mate = r + 1 - 2 * side
    right_mate = NY - 1 - r
    base = r - side

    def load(i, src, dst):
        return pltpu.make_async_copy(src, dst, in_sem.at[i])

    loads = (
        load(0, grad, gv),
        load(1, root_l, rlv.at[side]),
        load(2, root_r, rrv.at[0]),
        load(3, m1, m1v),
        load(4, m2, m2v),
        load(5, stat_l, slv),
        load(6, stat_r, srv),
    )
    for copy in loads:
        copy.start()

    barrier = pltpu.get_barrier_semaphore()

    def at(dx, dz, other=0):
        there = lax.rem(x + dx + NX, NX) * GROUP + lax.rem(z + dz + NZ, NZ) * NC
        return (r, there + lax.rem(c + other, NC))

    hellos = [(lax.rem(r + step, NY), s) for step in range(1, NY)]
    hellos += [at(dx, 0, other) for dx in range(NX) for other in range(NC) if dx or other]
    hellos += [at(0, 1), at(0, -1)]
    for device in hellos:
        pl.semaphore_signal(barrier, inc=1, device_id=device, device_id_type=MESH)

    lanes = lax.broadcasted_iota(jnp.int32, (8, 128), 1)
    blocks = jnp.full((8, 128), -1, jnp.int32)
    for b in range(nblk):
        blocks = jnp.where(lanes == owner[b], b, blocks)
    invv[...] = blocks
    invert = pltpu.make_async_copy(invv, inv, inv_sem)
    invert.start()
    loads[0].wait()
    invert.wait()

    def pick(slot, carry):
        outb[slot] = gv[jnp.maximum(inv[0, slot], 0)]
        return carry

    lax.fori_loop(0, NS, pick, 0, unroll=4)
    loads[1].wait()
    loads[2].wait()
    pl.semaphore_wait(barrier, len(hellos))

    mine = gc.at[r, x, rows_of(zc, 16)]
    pltpu.make_async_copy(outb.at[s], mine, bulk_recv.at[z]).start()

    def send_rows(dz):
        there = lax.rem(z + dz, NZ) * NC

        def body(i, carry):
            peer = lax.rem(x + lax.div(i, NC), NX) * GROUP + there + lax.rem(c + i, NC)
            remote(outb.at[peer], mine, bulk_send, bulk_recv.at[z], (r, peer)).start()
            return carry

        lax.fori_loop(1 if dz == 0 else 0, NX * NC, body, 0)

    quarters = [rows_of(lax.rem(lax.div(z, 2) + dq, 4), 64) for dq in Z_FAR]

    def left_root(j, i):
        ref = rlv.at[i, quarters[j]]
        return remote(ref, ref, l_send.at[j], l_recv.at[j], (left_mate, s))

    def right_root(j):
        rows = pl.ds(256 * j, 256)
        return remote(
            rrv.at[0, rows], rrv.at[1, rows], r_send.at[j], r_recv.at[j], (right_mate, s)
        )

    near = [lax.rem(z + NZ - dz, NZ) for dz in Z_NEAR]
    grads = ColumnGather(gc, [rows_of(other, 32) for other in near], (g_os, g_or, g_fs, g_fr), r, s)

    for j in range(4):
        right_root(j).start()
        left_root(j, side).start()

    loads[3].wait()
    loads[4].wait()

    def adam(b, carry):
        g = gv[b].astype(f32)
        first = beta_one * m1v[b] + (1.0 - beta_one) * g
        second = beta_two * m2v[b] + (1.0 - beta_two) * g * g
        m1v[b] = first
        m2v[b] = second
        step = first / (jnp.sqrt(second) + adam_eps)
        step = step * step
        step = step[:, :128] + step[:, 128:]
        acc[pl.ds(b, 1), :] = jnp.sum(step, axis=0, keepdims=True)
        return carry

    def say(i, device):
        pl.semaphore_signal(word.at[i], inc=1, device_id=device, device_id_type=MESH)

    def hear(i):
        pl.semaphore_wait(word.at[i], 1)

    say(0, at(0, 1))
    say(1, at(0, -1))
    send_rows(0)
    for step in range(1, 4):
        hear(2 * step - 2)
        hear(2 * step - 1)
        say(2 * step, at(0, 1))
        if step < 3:
            say(2 * step + 1, at(0, -1))
        send_rows(step)
        send_rows(NZ - step)
        lax.fori_loop((step - 1) * nblk // 3, step * nblk // 3, adam, 0, unroll=2)
    hear(6)
    send_rows(4)

    store_first = pltpu.make_async_copy(m1v, first_out, out_sem.at[0])
    store_second = pltpu.make_async_copy(m2v, second_out, out_sem.at[1])
    store_first.start()
    store_second.start()
    sums = jnp.sum(acc[...], axis=1, keepdims=True)
    lane = lax.broadcasted_iota(jnp.int32, (nblk, 128), 1)
    row = lax.broadcasted_iota(jnp.int32, (nblk, 128), 0)
    vec = jnp.sum(jnp.where(lane == row, sums, 0.0), axis=0, keepdims=True)
    vec = jnp.broadcast_to(vec, (8, 128))
    adam_sum = SmallSum(small_a, sa_send, sa_recv, r, s)
    adam_sum.start("core", vec)

    for k in range(NZ):
        await_bytes(grads.chunk(r, k), bulk_recv.at[near[k]])
        grads.send(k)
        if k >= LAG:
            grads.pass_on(k - LAG)
        if k == 1:
            adam_sum.start("z", adam_sum.finish("core"))
        if k == 4:
            adam_sum.start("x", adam_sum.finish("z"))
        if k == 6:
            adam_sum.start("y", adam_sum.finish("x"))
    for k in range(NZ - LAG, NZ):
        grads.pass_on(k)

    def right_rows(k):
        parts = [gc[q, :, grads.rows[k], :].reshape(NX * 32, 256) for q in range(NY)]
        for i, out in enumerate((tv, tv2)):
            total = jnp.zeros((NX * 32, 256), f32)
            for q in range(NY):
                total += jnp.dot(
                    parts[q], rrv[i, pl.ds(256 * q, 256), :], preferred_element_type=f32
                )
            out[:, grads.rows[k], :] = total.astype(bf16).reshape(NX, 32, 256)

    for j in range(4):
        right_root(j).wait_recv()
    for k in range(NZ):
        grads.last(k)
        right_rows(k)

    def give_back(plane, j):
        def body(i, carry):
            place = 4 * lax.rem(lax.div(z, 2) + Z_FAR[j], 4) + lax.rem(zc + i, 4)
            peer = plane * GROUP + place
            src = pv.at[plane, rows_of(place, 16)]
            dst = returned.at[s]

            @pl.when(peer != s)
            def _():
                remote(src, dst, back_send, back_recv, (r, peer)).start()

            @pl.when(peer == s)
            def _():
                pltpu.make_async_copy(src, dst, back_recv).start()

            return carry

        lax.fori_loop(0, 4, body, 0)

    def squares(part):
        wide = part.astype(f32)
        return jnp.sum(wide * wide, axis=0, keepdims=True)

    has = (inv[0, s] >= 0).astype(f32)

    def gram_left(j, carry):
        cols = rows_of(j, 256)
        total = jnp.zeros((256, 256), f32)
        for q in range(NY):
            total += lax.dot_general(
                gc[q, r], gc[q, j], (((1,), (1,)), ((), ())), preferred_element_type=f32
            )
        slv[:, cols] = slv[:, cols] + has * total
        return carry

    def gram_right(q, carry):
        cols = rows_of(q, 256)
        total = lax.dot_general(
            gc[r].reshape(1024, 256), gc[q].reshape(1024, 256), (((0,), (0,)), ((), ())),
            preferred_element_type=f32,
        )
        srv[:, cols] = srv[:, cols] + has * total
        return carry

    def product(left, right):
        return jnp.dot(
            left, right[...].reshape(1024, 256), preferred_element_type=f32
        ).astype(bf16)

    def shipment(i, j):
        plane = base + i
        return remote(
            ship.at[i, quarters[j]], pv.at[plane, quarters[j]], ship_send.at[i, j],
            ship_recv.at[i, j], (right_mate, s),
        )

    def shipped(i, j):
        plane = 2 - base + i
        await_bytes(pv.at[plane, quarters[j]], ship_recv.at[i, j])
        give_back(plane, j)

    for j in range(4):
        left_root(j, 1 - side).wait_recv()
    left = rlv[...].reshape(512, 1024)
    part = product(left, tv2)
    ship[0] = part[:256]
    ship[1] = part[256:]
    here = product(left, tv)
    pv[base] = here[:256]
    pv[base + 1] = here[256:]
    norm = squares(part) + squares(here)

    norm = jnp.sum(norm, axis=1, keepdims=True)
    spot = jnp.where(lanes == inv[0, s], jnp.broadcast_to(norm, (8, 128)), 0.0)
    norm_sum = SmallSum(small_p, sp_send, sp_recv, r, s)
    norm_sum.start("y", spot)
    for j in range(4):
        shipment(0, j).start()
        shipment(1, j).start()
    for j in range(2):
        give_back(base, j)
        give_back(base + 1, j)
    norms[s] = norm_sum.finish("y")[:1]

    def tell(i, carry):
        far = lax.rem(z + NZ // 2 + lax.div(i, NX * NC), NZ) * NC
        peer = lax.rem(x + 2 + lax.div(lax.rem(i, NX * NC), NC), NX) * GROUP + far + lax.rem(c + i, NC)
        ref = norms.at[s]

        @pl.when(peer != s)
        def _():
            remote(ref, ref, norm_send, norm_recv, (r, peer)).start()

        return carry

    lax.fori_loop(0, NS, tell, 0, unroll=4)
    for j in range(2, 4):
        give_back(base, j)
        give_back(base + 1, j)
    for j in range(2):
        shipped(0, j)
        shipped(1, j)
    loads[5].wait()
    lax.fori_loop(0, 4, gram_left, 0)
    store_left = pltpu.make_async_copy(slv, left_out, out_sem.at[2])
    store_left.start()
    for j in range(2, 4):
        shipped(0, j)
        shipped(1, j)

    loads[6].wait()
    lax.fori_loop(0, 4, gram_right, 0)
    store_right = pltpu.make_async_copy(srv, right_out, out_sem.at[3])
    store_right.start()

    grads.drain()
    for j in range(4):
        left_root(j, side).wait_send()
        right_root(j).wait_send()
        shipment(0, j).wait_send()
        shipment(1, j).wait_send()
    sent = outb.at[pl.ds(0, NS - 1)]
    await_bytes(sent, bulk_send)
    await_bytes(sent, back_send)
    adam_sq = adam_sum.finish("y")
    others = norms.at[pl.ds(0, NS - 1)]
    await_bytes(others, norm_send)
    await_bytes(others, norm_recv)
    norm_sq = jnp.sum(norms[...], axis=0)
    facv[...] = -(jnp.sqrt(adam_sq) / (jnp.sqrt(norm_sq) + norm_eps))
    store_factor = pltpu.make_async_copy(facv, factor_out, out_sem.at[4])
    store_factor.start()
    await_bytes(returned, back_recv)
    store_first.wait()
    store_second.wait()
    store_left.wait()
    store_right.wait()
    store_factor.wait()


def finish(
    owner, returned, factor, first, second, left, right,
    update_out, first_out, second_out, left_out, right_out,
    rows, facv, upv, m1v, m2v, slv, srv, in_sem, out_sem,
):
    chain = (
        (first, m1v, first_out), (second, m2v, second_out), (left, slv, left_out), (right, srv, right_out)
    )
    takes = [
        pltpu.make_async_copy(src, via, in_sem.at[2 + i]) for i, (src, via, _) in enumerate(chain)
    ]
    gives = [
        pltpu.make_async_copy(via, dst, out_sem.at[1 + i]) for i, (_, via, dst) in enumerate(chain)
    ]
    take = pltpu.make_async_copy(returned, rows, in_sem.at[0])
    take_factor = pltpu.make_async_copy(factor, facv, in_sem.at[1])
    take.start()
    take_factor.start()
    for copy in takes:
        copy.start()
    take_factor.wait()
    take.wait()
    scales = facv[...]
    for b in range(upv.shape[0]):
        scale = jnp.broadcast_to(scales[0:1, b : b + 1], upv.shape[1:])
        upv[b] = (scale * rows[owner[b]].astype(f32)).astype(bf16)
    give = pltpu.make_async_copy(upv, update_out, out_sem.at[0])
    give.start()
    for came, goes in zip(takes, gives):
        came.wait()
        goes.start()
    for copy in gives:
        copy.wait()
    give.wait()


def per_device(
    grad, first_moment, second_moment, stat_left, stat_right, root_left, root_right, owner_slot
):
    nblk, rows, cols = grad.shape
    span, width = stat_left.shape[1:]
    any_spec = pl.BlockSpec(memory_space=pl.ANY)
    smem_spec = pl.BlockSpec(memory_space=pltpu.SMEM)
    dma = pltpu.SemaphoreType.DMA
    moments = [jax.ShapeDtypeStruct(grad.shape, f32)] * 2
    stats = [jax.ShapeDtypeStruct((span, width), f32)] * 2
    grant = 60 * 1024 * 1024
    results = pl.pallas_call(
        kernel,
        out_shape=(
            jax.ShapeDtypeStruct((NS, rows, cols), bf16),
            jax.ShapeDtypeStruct((8, 128), f32),
            *moments,
            *stats,
        ),
        in_specs=[smem_spec] + [any_spec] * 7,
        out_specs=[any_spec] * 6,
        scratch_shapes=[
            pltpu.VMEM((nblk, rows, cols), bf16),
            pltpu.VMEM((nblk, rows, cols), f32),
            pltpu.VMEM((nblk, rows, cols), f32),
            pltpu.VMEM((span, width), f32),
            pltpu.VMEM((span, width), f32),
            pltpu.VMEM((2, span, width), bf16),
            pltpu.VMEM((2, width, cols), bf16),
            pltpu.VMEM((NS, rows, cols), bf16),
            pltpu.VMEM((NY, NX, width // NX, cols), bf16),
            pltpu.VMEM((NX, width // NX, cols), bf16),
            pltpu.VMEM((NX, width // NX, cols), bf16),
            pltpu.VMEM((NX, width // NX, cols), bf16),
            pltpu.VMEM((2, width // NX, cols), bf16),
            pltpu.VMEM((nblk, 128), f32),
            pltpu.VMEM((SMALL, 8, 128), f32),
            pltpu.VMEM((SMALL, 8, 128), f32),
            pltpu.VMEM((NS, 1, 128), f32),
            pltpu.VMEM((8, 128), f32),
            pltpu.VMEM((8, 128), jnp.int32),
            pltpu.SMEM((8, 128), jnp.int32),
            dma,
            pltpu.SemaphoreType.REGULAR((7,)),
            dma((7,)),
            dma((5,)),
            dma,
            dma((NZ,)),
            dma,
            dma,
            dma((2, NZ)),
            dma((2, NZ)),
            dma((NZ,)),
            dma((NZ,)),
            *[dma((4,))] * 4,
            *[dma((2, 4))] * 2,
            dma((4,)),
            dma((4,)),
            dma((4,)),
            dma((4,)),
            dma,
            dma,
        ],
        compiler_params=pltpu.CompilerParams(
            collective_id=0, has_side_effects=True, vmem_limit_bytes=grant
        ),
    )(
        owner_slot, grad, first_moment, second_moment, stat_left[0], stat_right[0],
        root_left[0], root_right[0],
    )
    update, first, second, left, right = pl.pallas_call(
        finish,
        out_shape=(jax.ShapeDtypeStruct(grad.shape, bf16), *moments, *stats),
        in_specs=[smem_spec] + [any_spec] * 6,
        out_specs=[any_spec] * 5,
        scratch_shapes=[
            pltpu.VMEM((NS, rows, cols), bf16),
            pltpu.VMEM((8, 128), f32),
            pltpu.VMEM((nblk, rows, cols), bf16),
            pltpu.VMEM((nblk, rows, cols), f32),
            pltpu.VMEM((nblk, rows, cols), f32),
            pltpu.VMEM((span, width), f32),
            pltpu.VMEM((span, width), f32),
            dma((6,)),
            dma((5,)),
        ],
        compiler_params=pltpu.CompilerParams(vmem_limit_bytes=grant),
    )(owner_slot, *results)
    return (update, first, second, left[None], right[None])


def solution(mesh):
    placed = (
        P(None, "shard", "rep"),
        P(None, "shard", "rep"),
        P(None, "shard", "rep"),
        P("shard", "rep", None),
        P("shard", "rep", None),
        P("shard", "rep", None),
        P("shard", None, "rep"),
        P(),
    )
    return jax.shard_map(
        per_device,
        mesh=mesh,
        in_specs=placed,
        out_specs=(
            P(None, "shard", "rep"),
            P(None, "shard", "rep"),
            P(None, "shard", "rep"),
            P("shard", "rep", None),
            P("shard", "rep", None),
        ),
        check_vma=False,
    )
```
